32 devices in a mesh: fsdp: 8 (over z, y), seq: 4 (over x, core).
Axes of the slice: x: 2, y: 2, z: 4, core: 2. Of those that a mesh axis runs over, the one named last changes fastest.
Arguments:
- hidden_in: bfloat16 [3, 4096, 768], P(None, ('fsdp', 'seq')), may hold values from -6 to 6
- row_types: int32 [3, 4096], P(None, ('fsdp', 'seq')), may hold values from 0 to 159, as said below
- lengths: int32 [3, 8, 8], P(None, 'fsdp'), may hold values from 1 to 384, as said below
- noise_time: float32 [3, 8, 8], P(None, 'fsdp'), may hold values from 0 to 1
- coords: float32 [3, 3, 4096], P(None, None, 'fsdp'), may hold values from -15 to 15
- residue_table: bfloat16 [32, 768], P(None, 'fsdp'), may hold values from -6 to 6
- atom_table: bfloat16 [128, 768], P(None, 'fsdp'), may hold values from -6 to 6
- time_weight: bfloat16 [768, 768], P('fsdp'), may hold values from -0.21875 to 0.21875
- first_gain: bfloat16 [768], P('fsdp'), may hold values from 0.25 to 1.75
- query_weight: bfloat16 [768, 768], P('fsdp'), may hold values from -0.21875 to 0.21875
- key_weight: bfloat16 [768, 768], P('fsdp'), may hold values from -0.21875 to 0.21875
- value_weight: bfloat16 [768, 768], P('fsdp'), may hold values from -0.21875 to 0.21875
- output_weight: bfloat16 [768, 768], P('fsdp'), may hold values from -1.75 to 1.75
- kernel_mean: bfloat16 [128], P('fsdp'), may hold values from 0.5 to 12
- kernel_width: bfloat16 [128], P('fsdp'), may hold values from 0.5 to 3
- pair_weight: bfloat16 [128, 32], P('fsdp'), may hold values from -12 to 12
- second_gain: bfloat16 [768], P('fsdp'), may hold values from 0.25 to 1.75
- up_weight: bfloat16 [768, 3072], P('fsdp'), may hold values from -0.21875 to 0.21875
- down_weight: bfloat16 [3072, 768], P('fsdp'), may hold values from -0.109375 to 0.109375
- force_weight: bfloat16 [3, 768], P(None, 'fsdp'), may hold values from -0.21875 to 0.21875
- layer_cot: bfloat16 [3, 4096, 768], P(None, ('fsdp', 'seq')), may hold values from -6 to 6
- force_cot: float32 [3, 3, 4096], P(None, None, ('fsdp', 'seq')), may hold values from -6 to 6
Outputs:
- layer_out: bfloat16 [3, 4096, 768], P(None, ('fsdp', 'seq'))
- forces: float32 [3, 3, 4096], P(None, None, ('fsdp', 'seq'))
- input_grad: float32 [3, 4096, 768], P(None, ('fsdp', 'seq'))
- residue_table_grad: float32 [32, 768], P(None, 'fsdp')
- atom_table_grad: float32 [128, 768], P(None, 'fsdp')
- time_weight_grad: float32 [768, 768], P('fsdp')
- first_gain_grad: float32 [768], P('fsdp')
- query_weight_grad: float32 [768, 768], P('fsdp')
- key_weight_grad: float32 [768, 768], P('fsdp')
- value_weight_grad: float32 [768, 768], P('fsdp')
- output_weight_grad: float32 [768, 768], P('fsdp')
- kernel_mean_grad: float32 [128], P('fsdp')
- kernel_width_grad: float32 [128], P('fsdp')
- pair_weight_grad: float32 [128, 32], P('fsdp')
- second_gain_grad: float32 [768], P('fsdp')
- up_weight_grad: float32 [768, 3072], P('fsdp')
- down_weight_grad: float32 [3072, 768], P('fsdp')
- force_weight_grad: float32 [3, 768], P(None, 'fsdp')
The draws below stay inside these ranges and needn't reach their ends.
Inputs may be any that keep to these rules, and one draw needn't show every extreme that they name: In each group, document 1 is a protein of exactly 384 rows, document 0 ends before row 128 of the group, all documents have at least one row, and the lengths of a group sum to 512. `row_types`: rows of document 1 hold a residue type below 32; all other rows hold 32 plus an atom type below 128.
All inputs are finite; a program needn't handle non-finite values.
Results may differ from the reference program's by a relative error of at most 0.019.
Values may be sent and summed in bfloat16 or wider, within the bound.
No kernel may reach another device: no remote copies, remote signals or barrier semaphores. Data moves between devices by JAX's collectives and lax.ppermute only.
A program may use at most 192 MiB of HBM per device.

```python
import math
import jax
import jax.numpy as jnp
from jax import lax

D = 768
HEADS = 32
FF = 3072
KERN = 128
RES_TYPES = 32
ATOM_TYPES = 128
NDOC = 8
MICRO = 3
TOK_DEV = 128
GROUP_ROWS = 512
GROUPS = 8
ROWS = 4096
LONGEST = 384


def group_layout(key):
    first_len = jax.random.randint(jax.random.fold_in(key, 11), (MICRO, GROUPS), 1, min(63, TOK_DEV - 6) + 1, dtype=jnp.int32)
    remaining = (GROUP_ROWS - LONGEST - first_len).astype(jnp.int32)
    base_len = remaining // 6
    extra_row = (jnp.arange(6, dtype=jnp.int32)[None, None, :] < (remaining % 6)[:, :, None]).astype(jnp.int32)
    shifts = jax.random.randint(jax.random.fold_in(key, 12), (MICRO, GROUPS, 6), 0, 4096, dtype=jnp.int32) % (base_len // 3 + 1)[:, :, None]
    molecules = base_len[:, :, None] + extra_row + shifts - jnp.roll(shifts, 1, axis=2)
    protein = jnp.full((MICRO, GROUPS, 1), LONGEST, jnp.int32)
    return jnp.concatenate([first_len[:, :, None], protein, molecules], axis=2).astype(jnp.int32)


def draw_lengths(key, part):
    shared = group_layout(key)
    return shared


def draw_row_types(key, part):
    doc_lengths = group_layout(key)
    key = jax.random.fold_in(key, 5)
    bounds = jnp.cumsum(doc_lengths, axis=2).astype(jnp.int32)
    row_ids = jnp.arange(GROUP_ROWS, dtype=jnp.int32)
    doc_ids = jnp.sum((row_ids[None, None, :, None] >= bounds[:, :, None, :]).astype(jnp.int32), axis=3)
    residues = jax.random.randint(jax.random.fold_in(key, 1), (MICRO, GROUPS, GROUP_ROWS), 0, RES_TYPES, dtype=jnp.int32)
    atoms = RES_TYPES + jax.random.randint(jax.random.fold_in(key, 2), (MICRO, GROUPS, GROUP_ROWS), 0, ATOM_TYPES, dtype=jnp.int32)
    return jnp.where(doc_ids == 1, residues, atoms).astype(jnp.int32).reshape(MICRO, GROUPS * GROUP_ROWS)


def block_scale(stream_key, dims, split, low, top_value):
    def one(position, blocks):
        heights = jax.random.uniform(jax.random.fold_in(jax.random.fold_in(stream_key, 6), position), (blocks,), jnp.float32, low / len(split), top_value / len(split))
        return jnp.repeat(jnp.exp(heights), dims[position] // blocks).reshape((-1,) + (1,) * (len(dims) - position - 1))

    level = one(*split[0])
    for cut in split[1:]:
        level = level * one(*cut)
    return level


def centred(own_key, shape, deviation, reach, split=(), kind=jnp.bfloat16):
    array = jax.random.normal(own_key, shape, jnp.float32) * deviation
    if len(split) > 0:
        array = block_scale(own_key, shape, split, -0.22, 0.18) * array
    return jnp.clip(array, min=-reach, max=reach).astype(kind)


def setup_inputs(seed: int = 0) -> dict:
    splits = jax.random.split(jax.random.key(seed), 23)
    hidden_in = centred(splits[0], (MICRO, ROWS, D), 1.0, 6.0, ((1, 32),))
    row_types = draw_row_types(jax.random.fold_in(splits[22], 71), 0)
    lengths = draw_lengths(jax.random.fold_in(splits[22], 71), 0)
    noise_time = jnp.clip(1.0 * jax.random.uniform(splits[3], (MICRO, GROUPS, NDOC), jnp.float32) ** block_scale(splits[3], (MICRO, GROUPS, NDOC), ((1, 8),), -0.2, 0.2), 0.0, 1.0)
    coords = centred(splits[4], (MICRO, 3, ROWS), 3.0, 15.0, ((2, 8),), jnp.float32)
    residue_table = centred(splits[5], (RES_TYPES, D), 1.0, 6.0, ((1, 8),))
    atom_table = centred(splits[6], (ATOM_TYPES, D), 1.0, 6.0, ((1, 8),))
    time_weight = centred(splits[7], (D, D), D ** -0.5, 0.21875, ((0, 8),))
    first_gain = jnp.clip(1.0 + 0.15 * jax.random.normal(splits[8], (D,), jnp.float32), 0.25, 1.75).astype(jnp.bfloat16)
    query_weight = centred(splits[9], (D, D), D ** -0.5, 0.21875, ((0, 8),))
    key_weight = centred(splits[10], (D, D), D ** -0.5, 0.21875, ((0, 8),))
    value_weight = centred(splits[11], (D, D), D ** -0.5, 0.21875, ((0, 8),))
    output_weight = centred(splits[12], (D, D), (D // 64) ** -0.5, 1.75, ((0, 8),))
    kernel_mean = jnp.clip(jnp.exp(math.log(12.0) - 3.1780538 * jax.random.uniform(splits[13], (KERN,), jnp.float32) ** block_scale(splits[13], (KERN,), ((0, 8),), -0.2, 0.2)), 0.5, 12.0).astype(jnp.bfloat16)
    kernel_width = jnp.clip(jnp.exp(math.log(3.0) - 1.7917595 * jax.random.uniform(splits[14], (KERN,), jnp.float32) ** block_scale(splits[14], (KERN,), ((0, 8),), -0.2, 0.2)), 0.5, 3.0).astype(jnp.bfloat16)
    pair_weight = centred(splits[15], (KERN, HEADS), 2.0, 12.0, ((0, 8),))
    second_gain = jnp.clip(1.0 + 0.15 * jax.random.normal(splits[16], (D,), jnp.float32), 0.25, 1.75).astype(jnp.bfloat16)
    up_weight = centred(splits[17], (D, FF), D ** -0.5, 0.21875, ((0, 8),))
    down_weight = centred(splits[18], (FF, D), FF ** -0.5, 0.109375, ((0, 8),))
    force_weight = centred(splits[19], (3, D), D ** -0.5, 0.21875, ((1, 8),))
    layer_cot = centred(splits[20], (MICRO, ROWS, D), 1.0, 6.0, ((1, 32),))
    force_cot = centred(splits[21], (MICRO, 3, ROWS), 1.0, 6.0, ((2, 32),), jnp.float32)
    return dict(hidden_in=hidden_in, row_types=row_types, lengths=lengths, noise_time=noise_time, coords=coords, residue_table=residue_table, atom_table=atom_table, time_weight=time_weight, first_gain=first_gain, query_weight=query_weight, key_weight=key_weight, value_weight=value_weight, output_weight=output_weight, kernel_mean=kernel_mean, kernel_width=kernel_width, pair_weight=pair_weight, second_gain=second_gain, up_weight=up_weight, down_weight=down_weight, force_weight=force_weight, layer_cot=layer_cot, force_cot=force_cot)


NORM_EPS = 1e-05
EXACT_PRECISION = lax.Precision.HIGHEST

@jax.custom_vjp
def low(v):
    return lax.optimization_barrier(v.astype(jnp.bfloat16)).astype(jnp.float32)

@jax.custom_vjp
def low_back(v):
    return v

def low_keep(v):
    return (low(v), None)

def low_pass(kept, grad):
    return (grad,)

def back_keep(v):
    return (v, None)

def back_low(kept, grad):
    return (low(grad),)
low.defvjp(low_keep, low_pass)
low_back.defvjp(back_keep, back_low)

def product(left, right):
    return jnp.dot(left, right, precision=EXACT_PRECISION)

def sinus_embed(stamps, model_width):
    half_width = model_width // 2
    frequency = jnp.exp(-math.log(10000.0) * jnp.arange(half_width).astype(jnp.float32) / half_width)
    angles = 1000.0 * stamps[:, None] * frequency[None, :]
    return jnp.concatenate([jnp.sin(angles), jnp.cos(angles)], axis=1)

def layer_norm(value, norm_gain):
    centre = value - lax.optimization_barrier(jnp.mean(value, axis=-1, keepdims=True))
    inv_std = lax.rsqrt(lax.optimization_barrier(jnp.mean(centre * centre, axis=-1, keepdims=True)) + NORM_EPS)
    return centre * inv_std * norm_gain

def gaussians(query_pos, key_pos, kernel_mean, kernel_width):
    delta_pos = query_pos[:, :, None] - key_pos[:, None, :]
    distance = jnp.sqrt(lax.optimization_barrier(jnp.sum(delta_pos * delta_pos, axis=0)))
    standard = (distance[:, :, None] - kernel_mean) / kernel_width
    return (jnp.exp(-0.5 * standard * standard) / (math.sqrt(2.0 * math.pi) * kernel_width), standard)

def attend_block(queries, query_pos, query_doc, keys_all, values_all, key_pos, key_doc, kernel_mean, kernel_width, pair_weight):
    row_count = queries.shape[0]
    head_count = pair_weight.shape[1]
    head_dim = queries.shape[1] // head_count
    density, _ = gaussians(query_pos, key_pos, kernel_mean, kernel_width)
    pair_bias = jnp.einsum('ijk,kh->hij', low(density), pair_weight, precision=EXACT_PRECISION)
    scores = jnp.einsum('ihd,jhd->hij', queries.reshape(row_count, head_count, head_dim), keys_all.reshape(-1, head_count, head_dim), precision=EXACT_PRECISION) * head_dim ** (-0.5)
    scores = low_back(scores + pair_bias)
    same_doc = query_doc[:, None] == key_doc[None, :]
    scores = jnp.where(same_doc[None], scores, -1000000000.0)
    maximum = lax.optimization_barrier(jnp.max(scores, axis=-1, keepdims=True))
    exp_scores = jnp.exp(scores - maximum)
    weights = low(exp_scores / lax.optimization_barrier(jnp.sum(exp_scores, axis=-1, keepdims=True)))
    attended = jnp.einsum('hij,jhd->ihd', weights, values_all.reshape(-1, head_count, head_dim), precision=EXACT_PRECISION)
    return attended.reshape(row_count, head_count * head_dim)

def layer(params, inputs, kinds, doc_lengths, stamps, positions):
    residue_table, atom_table, time_weight, first_gain, query_weight, key_weight, value_weight, output_weight, kernel_mean, kernel_width, pair_weight, second_gain, up_weight, down_weight, force_weight = params
    group_rows = inputs.shape[0]
    bounds = jnp.cumsum(doc_lengths).astype(jnp.int32)
    row_ids = jnp.arange(group_rows).astype(jnp.int32)
    doc_ids = lax.optimization_barrier(jnp.sum((row_ids[:, None] >= bounds[None, :]).astype(jnp.int32), axis=1)).astype(jnp.int32)
    doc_hot = (doc_ids[:, None] == jnp.arange(doc_lengths.shape[0]).astype(jnp.int32)[None, :]).astype(jnp.float32)
    residue_hot = (kinds[:, None] == jnp.arange(residue_table.shape[0]).astype(jnp.int32)[None, :]).astype(jnp.float32)
    atom_hot = ((kinds - residue_table.shape[0])[:, None] == jnp.arange(atom_table.shape[0]).astype(jnp.int32)[None, :]).astype(jnp.float32)
    time_proj = low_back(product(low(sinus_embed(stamps, inputs.shape[1])), time_weight))
    start_state = inputs + product(residue_hot, residue_table) + product(atom_hot, atom_table) + product(doc_hot, time_proj)
    attn_in = low(layer_norm(start_state, first_gain))
    queries = low(low_back(product(attn_in, query_weight)))
    keys_all = low(low_back(product(attn_in, key_weight)))
    values_all = low(low_back(product(attn_in, value_weight)))
    block_rows = min(128, group_rows)
    blocks = group_rows // block_rows

    def one_block(block_index):
        offset = (block_index * block_rows).astype(jnp.int32)
        return jax.checkpoint(attend_block)(lax.dynamic_slice_in_dim(queries, offset, block_rows, 0), lax.dynamic_slice_in_dim(positions, offset, block_rows, 1), lax.dynamic_slice_in_dim(doc_ids, offset, block_rows, 0), keys_all, values_all, positions, doc_ids, kernel_mean, kernel_width, pair_weight)
    attended = lax.map(one_block, jnp.arange(blocks).astype(jnp.int32)).reshape(group_rows, -1)
    attended = low(low_back(attended))
    mid_state = start_state + low_back(product(attended, output_weight))
    ffn_in = low(layer_norm(mid_state, second_gain))
    gelu_out = low(jax.nn.gelu(low_back(product(ffn_in, up_weight)), approximate=True))
    layer_out = low(mid_state + low_back(product(gelu_out, down_weight)))
    forces = product(force_weight, layer_out.T)
    return (layer_out, forces)

def reference(hidden_in, row_types, lengths, noise_time, coords, residue_table, atom_table, time_weight, first_gain, query_weight, key_weight, value_weight, output_weight, kernel_mean, kernel_width, pair_weight, second_gain, up_weight, down_weight, force_weight, layer_cot, force_cot):
    params = tuple((weight.astype(jnp.float32) for weight in (residue_table, atom_table, time_weight, first_gain, query_weight, key_weight, value_weight, output_weight, kernel_mean, kernel_width, pair_weight, second_gain, up_weight, down_weight, force_weight)))
    micro_count = hidden_in.shape[0]
    groups = lengths.shape[1]
    group_rows = hidden_in.shape[1] // groups
    model_width = hidden_in.shape[2]
    items = groups * micro_count
    records = (hidden_in.astype(jnp.float32).reshape(items, group_rows, model_width), row_types.reshape(items, group_rows), lengths.reshape(items, -1), noise_time.reshape(items, -1), coords.reshape(micro_count, 3, groups, group_rows).transpose(0, 2, 1, 3).reshape(items, 3, group_rows), layer_cot.astype(jnp.float32).reshape(items, group_rows, model_width), force_cot.reshape(micro_count, 3, groups, group_rows).transpose(0, 2, 1, 3).reshape(items, 3, group_rows))

    def group_step(grad_total, record):
        inputs, kinds, doc_lengths, stamps, positions, out_cot, forces_cot = record

        def forward(prm, source):
            return layer(prm, source, kinds, doc_lengths, stamps, positions)
        (layer_out, forces), pullback = jax.vjp(forward, params, inputs)
        param_grads, source_grad = pullback((out_cot, forces_cot))
        return (jax.tree.map(jnp.add, grad_total, param_grads), (layer_out.astype(jnp.bfloat16), forces, source_grad))
    zero_grads = jax.tree.map(jnp.zeros_like, params)
    totals, (outputs, force_rows, input_rows) = lax.scan(group_step, zero_grads, records)
    layer_out = outputs.reshape(micro_count, groups * group_rows, model_width)
    forces = force_rows.reshape(micro_count, groups, 3, group_rows).transpose(0, 2, 1, 3).reshape(micro_count, 3, groups * group_rows)
    input_grad = input_rows.reshape(micro_count, groups * group_rows, model_width)
    residue_grad, atom_grad, time_grad, first_grad, query_grad, key_grad, value_grad, output_grad, mean_grad, width_grad, pair_grad, second_grad, up_grad, down_grad, force_grad = totals
    return (layer_out, forces, input_grad, residue_grad, atom_grad, time_grad, first_grad, query_grad, key_grad, value_grad, output_grad, mean_grad, width_grad, pair_grad, second_grad, up_grad, down_grad, force_grad)
```

```python
import functools
import math

import jax
import jax.numpy as jnp
from jax import lax
from jax.experimental import pallas as pl
from jax.experimental.pallas import tpu as pltpu
from jax.sharding import PartitionSpec as P

NORM_EPS = 1e-05
PROTEIN_ROWS = 384
LANES = 128
HEAD_PAD = 32
TILE_ROWS = 8
LOG2E = math.log2(math.e)
VMEM_LIMIT = 56 * 2**20
EXACT = lax.Precision.HIGHEST
bf16 = jnp.bfloat16
f32 = jnp.float32


def dot_wide(left, right):
    return jnp.dot(left, right, preferred_element_type=f32)


def dot_tn(left, right):
    return lax.dot_general(left, right, (((0,), (0,)), ((), ())), preferred_element_type=f32)


def dot_nt(left, right):
    return lax.dot_general(left, right, (((1,), (1,)), ((), ())), preferred_element_type=f32)


def sinus_embed(stamps, model_width):
    half_width = model_width // 2
    frequency = jnp.exp(-math.log(10000.0) * jnp.arange(half_width).astype(f32) / half_width)
    angles = 1000.0 * stamps[..., None] * frequency
    return jnp.concatenate([jnp.sin(angles), jnp.cos(angles)], axis=-1)


def norm_forward(value, norm_gain):
    centre = value - jnp.mean(value, axis=-1, keepdims=True)
    inv_std = lax.rsqrt(jnp.mean(centre * centre, axis=-1, keepdims=True) + NORM_EPS)
    normed = centre * inv_std
    return normed * norm_gain, normed, inv_std


def norm_backward(grad_out, normed, inv_std, norm_gain):
    scaled = grad_out * norm_gain
    grad_in = inv_std * (
        scaled
        - jnp.mean(scaled, axis=-1, keepdims=True)
        - normed * jnp.mean(scaled * normed, axis=-1, keepdims=True)
    )
    return grad_in, jnp.sum(grad_out * normed, axis=0)


def density_rows(spans, mean_ref, coef_ref, powers):
    kernels = mean_ref.shape[0]
    tiles = spans[0].shape[1] // LANES
    parts = [[] for _ in range(powers)]
    for start in range(0, kernels, 16):
        mean = mean_ref[start : start + 16, :]
        coef = coef_ref[start : start + 16, :]
        pieces = [[] for _ in range(powers)]
        for span in spans:
            for tile in range(tiles):
                shift = span[:, tile * LANES : (tile + 1) * LANES] - mean
                dens = jnp.exp2(shift * shift * coef).astype(bf16)
                pieces[0].append(dens)
                if powers > 1:
                    low = shift.astype(bf16)
                    once = dens * low
                    pieces[1].append(once)
                    pieces[2].append(once * low)
        for power in range(powers):
            parts[power].append(jnp.concatenate(pieces[power], axis=1))
    return jnp.concatenate([piece for part in parts for piece in part], axis=0)


def bias_kernel(flag_ref, dist_ref, mask_ref, mean_ref, coef_ref, weight_ref, out_ref):
    micro = pl.program_id(0)
    row_count, columns = dist_ref.shape
    heads = weight_ref.shape[0]
    long_tiles = PROTEIN_ROWS // LANES
    all_tiles = columns // LANES

    def fill(base, first, tiles):
        empty = jnp.full((TILE_ROWS, LANES), -1e30, f32)
        for tile in range(first, first + tiles):
            for head in range(heads):
                out_ref[tile, pl.ds(head * row_count + base, TILE_ROWS), :] = empty

    def compute(base, first, tiles, batch):
        span = slice(first * LANES, (first + tiles) * LANES)
        dist = dist_ref[pl.ds(base, TILE_ROWS), span]
        mask = mask_ref[pl.ds(base, TILE_ROWS), span]
        for start in range(0, TILE_ROWS, batch):
            rows = range(start, start + batch)
            dens = density_rows([dist[row : row + 1] for row in rows], mean_ref, coef_ref, 1)
            bias = dot_wide(weight_ref[...], dens)
            for row in rows:
                for tile in range(tiles):
                    at = ((row - start) * tiles + tile) * LANES
                    out_ref[first + tile, pl.ds(base + row, heads, stride=row_count), :] = (
                        bias[:, at : at + LANES]
                        + mask[row : row + 1, tile * LANES : (tile + 1) * LANES]
                    )

    def one_tile(tile_index, carry):
        base = pl.multiple_of(tile_index * TILE_ROWS, TILE_ROWS)
        flag = flag_ref[micro, tile_index]

        @pl.when(flag != 1)
        def _():
            compute(base, 0, long_tiles, 2)

        @pl.when(flag == 1)
        def _():
            fill(base, 0, long_tiles)

        @pl.when(flag != 0)
        def _():
            compute(base, long_tiles, all_tiles - long_tiles, TILE_ROWS)

        @pl.when(flag == 0)
        def _():
            fill(base, long_tiles, all_tiles - long_tiles)

        return carry

    lax.fori_loop(0, row_count // TILE_ROWS, one_tile, 0)


def pair_bias(flags, dist, mask, mean_wide, coef_wide, weight):
    micro_count, row_count, columns = dist.shape
    heads, kernels = weight.shape
    block = pl.BlockSpec((None, row_count, columns), lambda m: (m, 0, 0))
    wide = pl.BlockSpec((kernels, LANES), lambda m: (0, 0))
    return pl.pallas_call(
        bias_kernel,
        grid=(micro_count,),
        in_specs=[
            pl.BlockSpec(memory_space=pltpu.SMEM),
            block,
            block,
            wide,
            wide,
            pl.BlockSpec((heads, kernels), lambda m: (0, 0)),
        ],
        out_specs=pl.BlockSpec(
            (None, columns // LANES, heads * row_count, LANES), lambda m: (m, 0, 0, 0)
        ),
        out_shape=jax.ShapeDtypeStruct(
            (micro_count, columns // LANES, heads * row_count, LANES), f32
        ),
        compiler_params=pltpu.CompilerParams(vmem_limit_bytes=VMEM_LIMIT),
        name="pair_bias",
    )(flags, dist, mask, mean_wide, coef_wide, weight)


def pair_grad_kernel(flag_ref, dist_ref, score_ref, mean_ref, coef_ref, out_ref):
    micro = pl.program_id(0)
    row_count, columns = dist_ref.shape
    heads = score_ref.shape[1] // row_count
    long_tiles = PROTEIN_ROWS // LANES
    all_tiles = columns // LANES
    out_ref[...] = jnp.zeros_like(out_ref)

    def compute(base, first, tiles, batch):
        total = out_ref[...]
        span = slice(first * LANES, (first + tiles) * LANES)
        dist = dist_ref[pl.ds(base, TILE_ROWS), span]
        for start in range(0, TILE_ROWS, batch):
            rows = range(start, start + batch)
            dens = density_rows([dist[row : row + 1] for row in rows], mean_ref, coef_ref, 3)
            score = jnp.concatenate(
                [
                    score_ref[first + tile, pl.ds(base + row, heads, stride=row_count), :]
                    for row in rows
                    for tile in range(tiles)
                ],
                axis=1,
            ).astype(bf16)
            total = total + dot_nt(score, dens)
        out_ref[...] = total

    def one_tile(tile_index, carry):
        base = pl.multiple_of(tile_index * TILE_ROWS, TILE_ROWS)
        flag = flag_ref[micro, tile_index]

        @pl.when(flag != 1)
        def _():
            compute(base, 0, long_tiles, 2)

        @pl.when(flag != 0)
        def _():
            compute(base, long_tiles, all_tiles - long_tiles, TILE_ROWS)

        return carry

    lax.fori_loop(0, row_count // TILE_ROWS, one_tile, 0)


def pair_grads(flags, dist, score_cot, mean_wide, coef_wide):
    micro_count, row_count, columns = dist.shape
    kernels = mean_wide.shape[0]
    heads = score_cot.shape[2] // row_count
    wide = pl.BlockSpec((kernels, LANES), lambda m: (0, 0))
    return pl.pallas_call(
        pair_grad_kernel,
        grid=(micro_count,),
        in_specs=[
            pl.BlockSpec(memory_space=pltpu.SMEM),
            pl.BlockSpec((None, row_count, columns), lambda m: (m, 0, 0)),
            pl.BlockSpec((None,) + score_cot.shape[1:], lambda m: (m, 0, 0, 0)),
            wide,
            wide,
        ],
        out_specs=pl.BlockSpec((None, heads, 3 * kernels), lambda m: (m, 0, 0)),
        out_shape=jax.ShapeDtypeStruct((micro_count, heads, 3 * kernels), f32),
        compiler_params=pltpu.CompilerParams(vmem_limit_bytes=VMEM_LIMIT),
        name="pair_grads",
    )(flags, dist, score_cot, mean_wide, coef_wide)


def head_stack(tile):
    lane_head = lax.broadcasted_iota(jnp.int32, (1, LANES), 1) // HEAD_PAD
    return jnp.concatenate(
        [
            jnp.where(lane_head == head, tile, jnp.zeros_like(tile))
            for head in range(LANES // HEAD_PAD)
        ],
        axis=0,
    )


def head_merge(stacked, row_count):
    lane_head = lax.broadcasted_iota(jnp.int32, (1, LANES), 1) // HEAD_PAD
    merged = stacked[:row_count]
    for head in range(1, LANES // HEAD_PAD):
        merged = jnp.where(
            lane_head == head, stacked[head * row_count : (head + 1) * row_count], merged
        )
    return merged


def attend_kernel(scale, query_ref, key_ref, value_ref, bias_ref, prob_ref, out_ref):
    row_count = query_ref.shape[0]
    tiles = bias_ref.shape[0]
    scores = dot_nt(head_stack(query_ref[...]), key_ref[...]) * scale
    scores = scores + jnp.concatenate([bias_ref[tile] for tile in range(tiles)], axis=1)
    exps = jnp.exp2(scores - jnp.max(scores, axis=1, keepdims=True))
    probs = (exps * (1.0 / jnp.sum(exps, axis=1, keepdims=True))).astype(bf16)
    prob_ref[...] = probs
    out_ref[...] = head_merge(dot_wide(probs, value_ref[...]), row_count).astype(bf16)


def attend(query, key, value, bias, scale):
    micro_count, row_count, width = query.shape
    columns = key.shape[1]
    groups = width // LANES
    stack = (LANES // HEAD_PAD) * row_count
    own = pl.BlockSpec((None, row_count, LANES), lambda m, g: (m, 0, g))
    whole = pl.BlockSpec((None, columns, LANES), lambda m, g: (m, 0, g))
    return pl.pallas_call(
        functools.partial(attend_kernel, scale),
        grid=(micro_count, groups),
        in_specs=[
            own,
            whole,
            whole,
            pl.BlockSpec((None, columns // LANES, stack, LANES), lambda m, g: (m, 0, g, 0)),
        ],
        out_specs=[pl.BlockSpec((None, stack, columns), lambda m, g: (m, g, 0)), own],
        out_shape=[
            jax.ShapeDtypeStruct((micro_count, groups * stack, columns), bf16),
            jax.ShapeDtypeStruct((micro_count, row_count, width), bf16),
        ],
        compiler_params=pltpu.CompilerParams(vmem_limit_bytes=VMEM_LIMIT),
        name="attend",
    )(query, key, value, bias)


def attend_back_kernel(
    scale,
    query_ref,
    key_ref,
    value_ref,
    cot_ref,
    prob_ref,
    score_ref,
    query_cot_ref,
    key_cot_ref,
    value_cot_ref,
):
    row_count = query_ref.shape[0]
    tiles = score_ref.shape[0]
    cot_stack = head_stack(cot_ref[...])
    query_stack = head_stack(query_ref[...])
    low_probs = prob_ref[...]
    probs = low_probs.astype(f32)
    prob_cot = dot_nt(cot_stack, value_ref[...])
    weighted = probs * prob_cot
    score_cot = weighted - probs * jnp.sum(weighted, axis=1, keepdims=True)
    for tile in range(tiles):
        score_ref[tile] = score_cot[:, tile * LANES : (tile + 1) * LANES]
    low = score_cot.astype(bf16)
    query_cot_ref[...] = (head_merge(dot_wide(low, key_ref[...]), row_count) * scale).astype(bf16)
    key_cot_ref[...] = (dot_tn(low, query_stack) * scale).astype(bf16)
    value_cot_ref[...] = dot_tn(low_probs, cot_stack).astype(bf16)


def attend_back(query, key, value, cot, probs, scale):
    micro_count, row_count, width = query.shape
    columns = key.shape[1]
    groups = width // LANES
    stack = (LANES // HEAD_PAD) * row_count
    own = pl.BlockSpec((None, row_count, LANES), lambda m, g: (m, 0, g))
    whole = pl.BlockSpec((None, columns, LANES), lambda m, g: (m, 0, g))
    return pl.pallas_call(
        functools.partial(attend_back_kernel, scale),
        grid=(micro_count, groups),
        in_specs=[
            own,
            whole,
            whole,
            own,
            pl.BlockSpec((None, stack, columns), lambda m, g: (m, g, 0)),
        ],
        out_specs=[
            pl.BlockSpec((None, columns // LANES, stack, LANES), lambda m, g: (m, 0, g, 0)),
            own,
            whole,
            whole,
        ],
        out_shape=[
            jax.ShapeDtypeStruct((micro_count, columns // LANES, groups * stack, LANES), f32),
            jax.ShapeDtypeStruct((micro_count, row_count, width), bf16),
            jax.ShapeDtypeStruct((micro_count, columns, width), bf16),
            jax.ShapeDtypeStruct((micro_count, columns, width), bf16),
        ],
        compiler_params=pltpu.CompilerParams(vmem_limit_bytes=VMEM_LIMIT),
        name="attend_back",
    )(query, key, value, cot, probs)


def place_matrix(source, piece, padded):
    index = jnp.arange(source, dtype=jnp.int32)
    target = (index // piece) * padded + index % piece
    spots = jnp.arange(source // piece * padded, dtype=jnp.int32)
    return (target[:, None] == spots[None, :]).astype(bf16)


def dot_low(left, right):
    return jnp.dot(left, right, preferred_element_type=f32).astype(bf16)


def roll_rows(value, shift, axis):
    size = value.shape[axis]
    twice = jnp.concatenate([value, value], axis=axis)
    return lax.dynamic_slice_in_dim(twice, shift, size, axis)


def gather_shards(shard):
    return lax.all_gather(shard, "fsdp", axis=0, tiled=True)


def reduce_shards(grad):
    part = lax.psum_scatter(grad, "fsdp", scatter_dimension=0, tiled=True)
    return lax.psum(part, "seq").astype(f32)[0]


def body(
    hidden_in,
    row_types,
    lengths,
    noise_time,
    coords,
    residue_table,
    atom_table,
    time_weight,
    first_gain,
    query_weight,
    key_weight,
    value_weight,
    output_weight,
    kernel_mean,
    kernel_width,
    pair_weight,
    second_gain,
    up_weight,
    down_weight,
    force_weight,
    layer_cot,
    force_cot,
):
    seq_count = lax.axis_size("seq")
    fsdp_count = lax.axis_size("fsdp")
    seq_index = lax.axis_index("seq")
    micro_count, tok_rows, model_width = hidden_in.shape
    group_rows = tok_rows * seq_count
    own_kernels, head_count = pair_weight.shape
    kernels = own_kernels * fsdp_count
    head_dim = model_width // head_count
    inv_root = head_dim ** (-0.5)
    wide_heads = head_count * HEAD_PAD
    total_rows = micro_count * tok_rows
    residues, own_width = residue_table.shape
    types = residues + atom_table.shape[0]
    offset = seq_index * tok_rows

    small_rows = types + 16
    small = jnp.concatenate(
        [
            residue_table,
            atom_table,
            force_weight,
            first_gain[None],
            second_gain[None],
            jnp.zeros((small_rows - types - 5, own_width), bf16),
        ],
        axis=0,
    )
    small = jnp.pad(small, ((0, 0), (0, LANES - own_width)))
    kernel_rows = jnp.concatenate([pair_weight, kernel_mean[:, None], kernel_width[:, None]], axis=1)
    kernel_rows = jnp.pad(kernel_rows, ((0, 0), (0, LANES - head_count - 2)))
    small_all = lax.all_gather(jnp.concatenate([small, kernel_rows], axis=0), "fsdp", axis=0)
    kernel_all = small_all[:, small_rows:].reshape(kernels, LANES)
    pair_full = kernel_all[:, :head_count].astype(f32)
    mean_full = kernel_all[:, head_count].astype(f32)
    width_full = kernel_all[:, head_count + 1].astype(f32)
    spread = place_matrix(model_width, own_width, LANES)
    tables = dot_low(
        small_all[:, :small_rows].transpose(1, 0, 2).reshape(small_rows, fsdp_count * LANES),
        spread.T,
    )
    type_table = tables[:types]
    force_wide = tables[types : types + 3].astype(f32)
    gain_one = tables[types + 3].astype(f32)
    gain_two = tables[types + 4].astype(f32)

    time_full = gather_shards(time_weight)
    query_full = gather_shards(query_weight)
    key_full = gather_shards(key_weight)
    value_full = gather_shards(value_weight)
    output_full = gather_shards(output_weight)
    up_full = gather_shards(up_weight)
    down_full = gather_shards(down_weight)

    doc_lengths = lengths[:, 0]
    bounds = jnp.cumsum(doc_lengths, axis=1)
    first_len = doc_lengths[:, 0]
    all_rows = jnp.arange(group_rows, dtype=jnp.int32)
    key_doc = jnp.sum((all_rows[None, :, None] >= bounds[:, None, :]).astype(jnp.int32), axis=2)
    query_doc = lax.dynamic_slice_in_dim(key_doc, offset, tok_rows, 1)
    query_pos = lax.dynamic_slice_in_dim(coords, offset, tok_rows, 2)
    roll_index = (all_rows[None, :] + first_len[:, None]) % group_rows
    rolled_doc = jnp.sum(
        (roll_index[:, :, None] >= bounds[:, None, :]).astype(jnp.int32), axis=2
    )
    rolled_pos = jnp.stack([roll_rows(coords[m], first_len[m], 1) for m in range(micro_count)])
    same_doc = query_doc[:, :, None] == rolled_doc[:, None, :]
    mask = jnp.where(same_doc, 0.0, -1e30).astype(f32)
    delta = query_pos[:, :, :, None] - rolled_pos[:, :, None, :]
    dist = jnp.sqrt(jnp.sum(delta * delta, axis=1))
    long_row = (query_doc == 1).reshape(micro_count, tok_rows // TILE_ROWS, TILE_ROWS)
    flags = jnp.where(
        jnp.all(long_row, axis=2), 0, jnp.where(jnp.any(long_row, axis=2), 2, 1)
    ).astype(jnp.int32)

    scale_k = 1.0 / (math.sqrt(2.0 * math.pi) * width_full)
    coef = (-0.5 * LOG2E) / (width_full * width_full)
    mean_wide = jnp.broadcast_to(mean_full[:, None], (kernels, LANES))
    coef_wide = jnp.broadcast_to(coef[:, None], (kernels, LANES))
    bias_weight = (pair_full * (scale_k * LOG2E)[:, None]).T.astype(bf16)
    bias = pair_bias(flags, dist, mask, mean_wide, coef_wide, bias_weight)

    doc_hot = (
        query_doc[:, :, None] == jnp.arange(doc_lengths.shape[1], dtype=jnp.int32)
    ).astype(f32)
    type_hot = (
        row_types.reshape(total_rows)[:, None] == jnp.arange(types, dtype=jnp.int32)
    ).astype(bf16)
    time_low = sinus_embed(noise_time[:, 0], model_width).astype(bf16)
    time_proj = dot_wide(time_low.reshape(-1, model_width), time_full).reshape(
        micro_count, -1, model_width
    )
    start_state = (
        hidden_in.astype(f32)
        + dot_wide(type_hot, type_table).reshape(hidden_in.shape)
        + jnp.einsum("min,mnd->mid", doc_hot, time_proj, precision=EXACT)
    ).reshape(total_rows, model_width)
    normed_in, normed_one, inv_one = norm_forward(start_state, gain_one)
    attn_in = normed_in.astype(bf16)

    head_place = place_matrix(model_width, head_dim, HEAD_PAD)
    query_pad = dot_low(query_full, head_place)
    key_pad = dot_low(key_full, head_place)
    value_pad = dot_low(value_full, head_place)
    output_pad = dot_low(head_place.T, output_full)
    attn_all = lax.all_gather(
        attn_in.reshape(micro_count, tok_rows, model_width), "seq", axis=1, tiled=True
    )
    attn_all = jnp.concatenate(
        [roll_rows(attn_all[m], first_len[m], 0) for m in range(micro_count)], axis=0
    )
    queries = dot_low(attn_in, query_pad).reshape(micro_count, tok_rows, wide_heads)
    keys = dot_low(attn_all, key_pad).reshape(micro_count, group_rows, wide_heads)
    values = dot_low(attn_all, value_pad).reshape(micro_count, group_rows, wide_heads)
    probs, attended = attend(queries, keys, values, bias, inv_root * LOG2E)
    attended = attended.reshape(total_rows, wide_heads)

    mid_state = start_state + dot_wide(attended, output_pad)
    normed_mid, normed_two, inv_two = norm_forward(mid_state, gain_two)
    ffn_in = normed_mid.astype(bf16)
    up_state = dot_wide(ffn_in, up_full)
    gelu_low = jax.nn.gelu(up_state, approximate=True).astype(bf16)
    layer_out = (mid_state + dot_wide(gelu_low, down_full)).astype(bf16)
    forces = dot_nt(force_wide.astype(bf16), layer_out)
    forces = forces.reshape(3, micro_count, tok_rows).transpose(1, 0, 2)

    forces_cot = force_cot.transpose(1, 0, 2).reshape(3, total_rows)
    out_grad = layer_cot.reshape(total_rows, model_width).astype(f32)
    for axis in range(3):
        out_grad = out_grad + forces_cot[axis][:, None] * force_wide[axis][None, :]
    force_w_grad = jnp.dot(forces_cot, layer_out.astype(f32), precision=EXACT)
    branch_low = out_grad.astype(bf16)
    down_w_grad = dot_tn(gelu_low, branch_low)
    gelu_grad = dot_nt(branch_low, down_full)
    _, gelu_pull = jax.vjp(lambda inner: jax.nn.gelu(inner, approximate=True), up_state)
    up_low = gelu_pull(gelu_grad)[0].astype(bf16)
    up_w_grad = dot_tn(ffn_in, up_low)
    ffn_in_grad = dot_nt(up_low, up_full)
    norm_part, gain_two_grad = norm_backward(ffn_in_grad, normed_two, inv_two, gain_two)
    mid_grad = out_grad + norm_part
    attn_low = mid_grad.astype(bf16)
    output_w_grad = dot_low(head_place, dot_tn(attended, attn_low).astype(bf16))
    attended_grad = dot_nt(attn_low, output_pad).astype(bf16)

    score_cot, query_low, key_part, value_part = attend_back(
        queries,
        keys,
        values,
        attended_grad.reshape(micro_count, tok_rows, wide_heads),
        probs,
        inv_root,
    )
    query_low = query_low.reshape(total_rows, wide_heads)
    key_part = key_part.reshape(-1, wide_heads)
    value_part = value_part.reshape(-1, wide_heads)
    all_part = (dot_nt(key_part, key_pad) + dot_nt(value_part, value_pad)).astype(bf16)
    all_part = all_part.reshape(micro_count, group_rows, model_width)
    all_part = jnp.stack(
        [roll_rows(all_part[m], group_rows - first_len[m], 0) for m in range(micro_count)]
    )
    own_part = lax.psum_scatter(all_part, "seq", scatter_dimension=1, tiled=True)
    query_w_grad = dot_low(dot_tn(attn_in, query_low).astype(bf16), head_place.T)
    key_w_grad = dot_low(dot_tn(attn_all, key_part).astype(bf16), head_place.T)
    value_w_grad = dot_low(dot_tn(attn_all, value_part).astype(bf16), head_place.T)
    attn_in_grad = dot_nt(query_low, query_pad) + own_part.reshape(
        total_rows, model_width
    ).astype(f32)
    norm_part_one, gain_one_grad = norm_backward(attn_in_grad, normed_one, inv_one, gain_one)
    input_grad = mid_grad + norm_part_one

    input_low = input_grad.astype(bf16)
    type_grad = dot_tn(type_hot, input_low)
    time_cot = jnp.einsum(
        "min,mid->mnd",
        doc_hot.astype(bf16),
        input_low.reshape(micro_count, tok_rows, model_width),
        preferred_element_type=f32,
    ).astype(bf16)
    time_w_grad = dot_tn(
        time_low.reshape(-1, model_width), time_cot.reshape(-1, model_width)
    ).astype(bf16)

    sums = jnp.sum(pair_grads(flags, dist, score_cot, mean_wide, coef_wide), axis=0)
    plain, once, twice = (sums[:, k * kernels : (k + 1) * kernels].T for k in range(3))
    pair_w_grad = plain * scale_k[:, None]
    inv_width = 1.0 / width_full
    mean_grad = jnp.sum(pair_full * once, axis=1) * scale_k * inv_width * inv_width
    width_grad = (
        jnp.sum(pair_full * (twice * (inv_width * inv_width)[:, None] - plain), axis=1)
        * scale_k
        * inv_width
    )

    def by_shard(grad):
        return grad.reshape(fsdp_count, -1, grad.shape[-1]).astype(bf16)

    small_grad = jnp.concatenate(
        [
            type_grad,
            force_w_grad,
            gain_one_grad[None],
            gain_two_grad[None],
            jnp.zeros((small_rows - types - 5, model_width), f32),
        ],
        axis=0,
    )
    small_grad = dot_low(small_grad.astype(bf16), spread)
    small_grad = small_grad.reshape(small_rows, fsdp_count, LANES).transpose(1, 0, 2)
    kernel_grad = jnp.concatenate(
        [pair_w_grad, mean_grad[:, None], width_grad[:, None]], axis=1
    ).astype(bf16)
    kernel_grad = jnp.pad(kernel_grad, ((0, 0), (0, LANES - head_count - 2)))
    small_grad = jnp.concatenate(
        [small_grad, kernel_grad.reshape(fsdp_count, own_kernels, LANES)], axis=1
    )
    down_sum = reduce_shards(by_shard(down_w_grad))
    up_sum = reduce_shards(by_shard(up_w_grad))
    output_sum = reduce_shards(by_shard(output_w_grad))
    query_sum = reduce_shards(by_shard(query_w_grad))
    key_sum = reduce_shards(by_shard(key_w_grad))
    value_sum = reduce_shards(by_shard(value_w_grad))
    time_sum = reduce_shards(by_shard(time_w_grad))
    small_sum = reduce_shards(small_grad)
    kernel_sum = small_sum[small_rows:]
    row_sum = small_sum[:small_rows, :own_width]
    return (
        layer_out.reshape(hidden_in.shape),
        forces,
        input_grad.reshape(hidden_in.shape),
        row_sum[:residues],
        row_sum[residues:types],
        time_sum,
        row_sum[types + 3],
        query_sum,
        key_sum,
        value_sum,
        output_sum,
        kernel_sum[:, head_count],
        kernel_sum[:, head_count + 1],
        kernel_sum[:, :head_count],
        row_sum[types + 4],
        up_sum,
        down_sum,
        row_sum[types : types + 3],
    )


def solution(mesh):
    rows = ("fsdp", "seq")
    return jax.shard_map(
        body,
        mesh=mesh,
        in_specs=(
            P(None, rows, None),
            P(None, rows),
            P(None, "fsdp", None),
            P(None, "fsdp", None),
            P(None, None, "fsdp"),
            P(None, "fsdp"),
            P(None, "fsdp"),
            P("fsdp", None),
            P("fsdp"),
            P("fsdp", None),
            P("fsdp", None),
            P("fsdp", None),
            P("fsdp", None),
            P("fsdp"),
            P("fsdp"),
            P("fsdp", None),
            P("fsdp"),
            P("fsdp", None),
            P("fsdp", None),
            P(None, "fsdp"),
            P(None, rows, None),
            P(None, None, rows),
        ),
        out_specs=(
            P(None, rows, None),
            P(None, None, rows),
            P(None, rows, None),
            P(None, "fsdp"),
            P(None, "fsdp"),
            P("fsdp", None),
            P("fsdp"),
            P("fsdp", None),
            P("fsdp", None),
            P("fsdp", None),
            P("fsdp", None),
            P("fsdp"),
            P("fsdp"),
            P("fsdp", None),
            P("fsdp"),
            P("fsdp", None),
            P("fsdp", None),
            P(None, "fsdp"),
        ),
        check_vma=False,
    )
```

```python
import functools
import math

import jax
import jax.numpy as jnp
from jax import lax
from jax.experimental import pallas as pl
from jax.experimental.pallas import tpu as pltpu
from jax.sharding import PartitionSpec as P

NORM_EPS = 1e-05
PROTEIN_ROWS = 384
LANES = 128
HEAD_PAD = 32
TILE_ROWS = 8
ROW_BLOCK = 32
CENTRE = 6.0
PER_STEP = 4
LOG2E = math.log2(math.e)
VMEM_LIMIT = 56 * 2**20
EXACT = lax.Precision.HIGHEST
bf16 = jnp.bfloat16
f32 = jnp.float32


def dot_wide(left, right):
    return jnp.dot(left, right, preferred_element_type=f32)


def dot_tn(left, right):
    return lax.dot_general(left, right, (((0,), (0,)), ((), ())), preferred_element_type=f32)


def dot_nt(left, right):
    return lax.dot_general(left, right, (((1,), (1,)), ((), ())), preferred_element_type=f32)


def cost(micros):
    return pl.CostEstimate(flops=int(micros * 0.04e9), bytes_accessed=0, transcendentals=0)


def sinus_columns(stamps, model_width, first, columns):
    half_width = model_width // 2
    index = first + jnp.arange(columns, dtype=jnp.int32)
    step = (index % half_width).astype(f32)
    frequency = jnp.exp(-math.log(10000.0) * step / half_width)
    angles = 1000.0 * stamps[..., None] * frequency
    return jnp.where(index < half_width, jnp.sin(angles), jnp.cos(angles)).astype(bf16)


def norm_forward(value, norm_gain):
    centre = value - jnp.mean(value, axis=-1, keepdims=True)
    inv_std = lax.rsqrt(jnp.mean(centre * centre, axis=-1, keepdims=True) + NORM_EPS)
    normed = centre * inv_std
    return normed * norm_gain, normed, inv_std


def norm_backward(grad_out, normed, inv_std, norm_gain):
    scaled = grad_out * norm_gain
    grad_in = inv_std * (
        scaled
        - jnp.mean(scaled, axis=-1, keepdims=True)
        - normed * jnp.mean(scaled * normed, axis=-1, keepdims=True)
    )
    return grad_in, jnp.sum(grad_out * normed, axis=0)


def density_rows(spans, mean_ref, coef_ref, base_ref):
    kernels = mean_ref.shape[0]
    tiles = spans[0].shape[1] // LANES
    parts = []
    for start in range(0, kernels, 16):
        mean = mean_ref[start : start + 16, :]
        coef = coef_ref[start : start + 16, :]
        pieces = []
        for span in spans:
            for tile in range(tiles):
                shift = span[:, tile * LANES : (tile + 1) * LANES] - mean
                power = shift * shift * coef
                if base_ref is not None:
                    power = power + base_ref[start : start + 16, :]
                pieces.append(jnp.exp2(power).astype(bf16))
        parts.append(jnp.concatenate(pieces, axis=1))
    return jnp.concatenate(parts, axis=0)


def bias_kernel(
    micro, flag_ref, dist_ref, mask_ref, mean_ref, coef_ref, base_ref, weight_ref, *rest
):
    out_ref = rest[-1]
    row_count, columns = dist_ref.shape
    heads = weight_ref.shape[0]
    long_tiles = PROTEIN_ROWS // LANES
    all_tiles = columns // LANES

    def fill(base, first, tiles):
        empty = jnp.full((TILE_ROWS, LANES), -1e30, f32)
        for tile in range(first, first + tiles):
            for head in range(heads):
                out_ref[tile, pl.ds(head * row_count + base, TILE_ROWS), :] = empty

    def compute(base, first, tiles, batch):
        span = slice(first * LANES, (first + tiles) * LANES)
        dist = dist_ref[pl.ds(base, TILE_ROWS), span]
        mask = mask_ref[pl.ds(base, TILE_ROWS), span]
        for start in range(0, TILE_ROWS, batch):
            rows = range(start, start + batch)
            dens = density_rows(
                [dist[row : row + 1] for row in rows], mean_ref, coef_ref, base_ref
            )
            bias = dot_wide(weight_ref[...], dens) * LOG2E
            for row in rows:
                for tile in range(tiles):
                    at = ((row - start) * tiles + tile) * LANES
                    out_ref[first + tile, pl.ds(base + row, heads, stride=row_count), :] = (
                        bias[:, at : at + LANES]
                        + mask[row : row + 1, tile * LANES : (tile + 1) * LANES]
                    )

    def one_tile(tile_index, carry):
        base = pl.multiple_of(tile_index * TILE_ROWS, TILE_ROWS)
        flag = flag_ref[micro, pl.program_id(0) * (row_count // TILE_ROWS) + tile_index]

        @pl.when(flag != 1)
        def _():
            compute(base, 0, long_tiles, 2)

        @pl.when(flag == 1)
        def _():
            fill(base, 0, long_tiles)

        @pl.when(flag != 0)
        def _():
            compute(base, long_tiles, all_tiles - long_tiles, TILE_ROWS)

        @pl.when(flag == 0)
        def _():
            fill(base, long_tiles, all_tiles - long_tiles)

        return carry

    lax.fori_loop(0, row_count // TILE_ROWS, one_tile, 0)


def pair_bias(micro, earlier, flags, dist, mask, mean_wide, coef_wide, base_wide, weight):
    micro_count, row_count, columns = dist.shape
    heads, kernels = weight.shape
    blocks = row_count // ROW_BLOCK
    block = pl.BlockSpec((None, ROW_BLOCK, columns), lambda i: (micro, i, 0))
    wide = pl.BlockSpec((kernels, LANES), lambda i: (0, 0))
    shape = (micro_count, blocks, columns // LANES, heads * ROW_BLOCK, LANES)
    operands = [flags, dist, mask, mean_wide, coef_wide, base_wide, weight]
    specs = [
        pl.BlockSpec(memory_space=pltpu.SMEM),
        block,
        block,
        wide,
        wide,
        wide,
        pl.BlockSpec((heads, kernels), lambda i: (0, 0)),
    ]
    if earlier is not None:
        operands.append(earlier)
        specs.append(pl.BlockSpec(memory_space=pl.ANY))
    return pl.pallas_call(
        functools.partial(bias_kernel, micro),
        grid=(blocks,),
        in_specs=specs,
        out_specs=pl.BlockSpec((None, None) + shape[2:], lambda i: (micro, i, 0, 0, 0)),
        out_shape=jax.ShapeDtypeStruct(shape, f32),
        input_output_aliases={} if earlier is None else {7: 0},
        compiler_params=pltpu.CompilerParams(vmem_limit_bytes=VMEM_LIMIT),
        cost_estimate=cost(11),
        name="pair_bias",
    )(*operands)


def two_parts(value):
    high = value.astype(bf16)
    return high, (value - high.astype(f32)).astype(bf16)


def pair_grad_kernel(micro, flag_ref, dist_ref, score_ref, mean_ref, coef_ref, out_ref):
    row_count, columns = dist_ref.shape
    heads = score_ref.shape[1] // row_count
    long_tiles = PROTEIN_ROWS // LANES
    all_tiles = columns // LANES

    @pl.when(pl.program_id(0) == 0)
    def _():
        out_ref[...] = jnp.zeros_like(out_ref)

    def compute(base, first, tiles, batch):
        total = out_ref[...]
        span = slice(first * LANES, (first + tiles) * LANES)
        dist = dist_ref[pl.ds(base, TILE_ROWS), span]
        for start in range(0, TILE_ROWS, batch):
            rows = range(start, start + batch)
            dens = density_rows([dist[row : row + 1] for row in rows], mean_ref, coef_ref, None)
            score = jnp.concatenate(
                [
                    score_ref[first + tile, pl.ds(base + row, heads, stride=row_count), :]
                    for row in rows
                    for tile in range(tiles)
                ],
                axis=1,
            ).astype(bf16)
            far = jnp.concatenate([dist[row : row + 1] for row in rows], axis=1) - CENTRE
            once = score.astype(f32) * far
            stack = jnp.concatenate([score, *two_parts(once), *two_parts(once * far)], axis=0)
            total = total + dot_nt(stack, dens)
        out_ref[...] = total

    def one_tile(tile_index, carry):
        base = pl.multiple_of(tile_index * TILE_ROWS, TILE_ROWS)
        flag = flag_ref[micro, pl.program_id(0) * (row_count // TILE_ROWS) + tile_index]

        @pl.when(flag != 1)
        def _():
            compute(base, 0, long_tiles, 2)

        @pl.when(flag != 0)
        def _():
            compute(base, long_tiles, all_tiles - long_tiles, TILE_ROWS)

        return carry

    lax.fori_loop(0, row_count // TILE_ROWS, one_tile, 0)


def pair_grads(micro, flags, dist, score_cot, mean_wide, coef_wide):
    columns = dist.shape[2]
    blocks = score_cot.shape[1]
    kernels = mean_wide.shape[0]
    heads = score_cot.shape[3] // ROW_BLOCK
    wide = pl.BlockSpec((kernels, LANES), lambda i: (0, 0))
    return pl.pallas_call(
        functools.partial(pair_grad_kernel, micro),
        grid=(blocks,),
        in_specs=[
            pl.BlockSpec(memory_space=pltpu.SMEM),
            pl.BlockSpec((None, ROW_BLOCK, columns), lambda i: (micro, i, 0)),
            pl.BlockSpec((None, None) + score_cot.shape[2:], lambda i: (micro, i, 0, 0, 0)),
            wide,
            wide,
        ],
        out_specs=pl.BlockSpec((5 * heads, kernels), lambda i: (0, 0)),
        out_shape=jax.ShapeDtypeStruct((5 * heads, kernels), f32),
        compiler_params=pltpu.CompilerParams(vmem_limit_bytes=VMEM_LIMIT),
        cost_estimate=cost(14),
        name="pair_grads",
    )(flags, dist, score_cot, mean_wide, coef_wide)


def head_stack(tile):
    lane_head = lax.broadcasted_iota(jnp.int32, (1, LANES), 1) // HEAD_PAD
    return jnp.concatenate(
        [
            jnp.where(lane_head == head, tile, jnp.zeros_like(tile))
            for head in range(LANES // HEAD_PAD)
        ],
        axis=0,
    )


def head_merge(stacked, row_count):
    lane_head = lax.broadcasted_iota(jnp.int32, (1, LANES), 1) // HEAD_PAD
    merged = stacked[:row_count]
    for head in range(1, LANES // HEAD_PAD):
        merged = jnp.where(
            lane_head == head, stacked[head * row_count : (head + 1) * row_count], merged
        )
    return merged


def attend_kernel(scale, query_ref, key_ref, value_ref, bias_ref, prob_ref, out_ref):
    row_count = query_ref.shape[0]
    blocks, tiles = bias_ref.shape[:2]
    heads = LANES // HEAD_PAD
    stack = heads * row_count
    for group in range(query_ref.shape[1] // LANES):
        lanes = slice(group * LANES, (group + 1) * LANES)
        rows = slice(group * stack, (group + 1) * stack)
        scores = dot_nt(head_stack(query_ref[:, lanes]), key_ref[:, lanes]) * scale
        bias = [
            [
                bias_ref[block, tile, head * ROW_BLOCK : (head + 1) * ROW_BLOCK]
                for head in range(group * heads, (group + 1) * heads)
                for block in range(blocks)
            ]
            for tile in range(tiles)
        ]
        scores = scores + jnp.concatenate([jnp.concatenate(b, axis=0) for b in bias], axis=1)
        exps = jnp.exp2(scores - jnp.max(scores, axis=1, keepdims=True))
        probs = (exps * (1.0 / jnp.sum(exps, axis=1, keepdims=True))).astype(bf16)
        prob_ref[rows] = probs
        merged = head_merge(dot_wide(probs, value_ref[:, lanes]), row_count)
        out_ref[:, lanes] = merged.astype(bf16)


def attend(query, both, bias, scale):
    micro_count, row_count, width = query.shape
    columns = both.shape[1]
    wide = PER_STEP * LANES
    groups = width // wide
    heads = PER_STEP * (LANES // HEAD_PAD)
    stack = heads * row_count
    own = pl.BlockSpec((None, row_count, wide), lambda m, g: (m, 0, g))
    whole = pl.BlockSpec((None, columns, wide), lambda m, g: (m, 0, g))
    later = pl.BlockSpec((None, columns, wide), lambda m, g: (m, 0, groups + g))
    return pl.pallas_call(
        functools.partial(attend_kernel, scale),
        grid=(micro_count, groups),
        in_specs=[
            own,
            whole,
            later,
            pl.BlockSpec(
                (None, row_count // ROW_BLOCK, columns // LANES, heads * ROW_BLOCK, LANES),
                lambda m, g: (m, 0, 0, g, 0),
            ),
        ],
        out_specs=[pl.BlockSpec((None, stack, columns), lambda m, g: (m, g, 0)), own],
        out_shape=[
            jax.ShapeDtypeStruct((micro_count, groups * stack, columns), bf16),
            jax.ShapeDtypeStruct((micro_count, row_count, width), bf16),
        ],
        compiler_params=pltpu.CompilerParams(vmem_limit_bytes=VMEM_LIMIT),
        cost_estimate=cost(30),
        name="attend",
    )(query, both, both, bias)


def attend_back_kernel(
    scale,
    query_ref,
    key_ref,
    value_ref,
    cot_ref,
    prob_ref,
    score_ref,
    query_cot_ref,
    key_cot_ref,
    value_cot_ref,
):
    row_count = query_ref.shape[0]
    blocks, tiles = score_ref.shape[:2]
    heads = LANES // HEAD_PAD
    stack = heads * row_count
    for group in range(query_ref.shape[1] // LANES):
        lanes = slice(group * LANES, (group + 1) * LANES)
        rows = slice(group * stack, (group + 1) * stack)
        cot_stack = head_stack(cot_ref[:, lanes])
        low_probs = prob_ref[rows]
        probs = low_probs.astype(f32)
        weighted = probs * dot_nt(cot_stack, value_ref[:, lanes])
        score_cot = weighted - probs * jnp.sum(weighted, axis=1, keepdims=True)
        for head in range(heads):
            to = slice((group * heads + head) * ROW_BLOCK, (group * heads + head + 1) * ROW_BLOCK)
            for block in range(blocks):
                at = head * row_count + block * ROW_BLOCK
                for tile in range(tiles):
                    score_ref[block, tile, to] = score_cot[
                        at : at + ROW_BLOCK, tile * LANES : (tile + 1) * LANES
                    ]
        low = score_cot.astype(bf16)
        merged = head_merge(dot_wide(low, key_ref[:, lanes]), row_count)
        query_cot_ref[:, lanes] = (merged * scale).astype(bf16)
        key_cot = dot_tn(low, head_stack(query_ref[:, lanes])) * scale
        key_cot_ref[:, lanes] = key_cot.astype(bf16)
        value_cot_ref[:, lanes] = dot_tn(low_probs, cot_stack).astype(bf16)


def attend_back(query, both, cot, probs, scale):
    micro_count, row_count, width = query.shape
    columns = both.shape[1]
    block = (
        row_count // ROW_BLOCK,
        columns // LANES,
        PER_STEP * (LANES // HEAD_PAD) * ROW_BLOCK,
        LANES,
    )
    wide = PER_STEP * LANES
    groups = width // wide
    heads = PER_STEP * (LANES // HEAD_PAD)
    stack = heads * row_count
    own = pl.BlockSpec((None, row_count, wide), lambda m, g: (m, 0, g))
    whole = pl.BlockSpec((None, columns, wide), lambda m, g: (m, 0, g))
    later = pl.BlockSpec((None, columns, wide), lambda m, g: (m, 0, groups + g))
    return pl.pallas_call(
        functools.partial(attend_back_kernel, scale),
        grid=(micro_count, groups),
        in_specs=[
            own,
            whole,
            later,
            own,
            pl.BlockSpec((None, stack, columns), lambda m, g: (m, g, 0)),
        ],
        out_specs=[
            pl.BlockSpec((None,) + block, lambda m, g: (m, 0, 0, g, 0)),
            own,
            whole,
            whole,
        ],
        out_shape=[
            jax.ShapeDtypeStruct(
                (micro_count,) + block[:2] + (groups * block[2], LANES), f32
            ),
            jax.ShapeDtypeStruct((micro_count, row_count, width), bf16),
            jax.ShapeDtypeStruct((micro_count, columns, width), bf16),
            jax.ShapeDtypeStruct((micro_count, columns, width), bf16),
        ],
        compiler_params=pltpu.CompilerParams(vmem_limit_bytes=VMEM_LIMIT),
        cost_estimate=cost(35),
        name="attend_back",
    )(query, both, both, cot, probs)


def spans(start, stop, width):
    pieces = []
    at = start
    while at < stop:
        block = at // width
        last = min(stop, (block + 1) * width)
        pieces.append((block, at - block * width, last - block * width, at - start))
        at = last
    return pieces


def roll_matrix(size, shift):
    row = lax.broadcasted_iota(jnp.int32, (size, size), 0) + shift
    row = jnp.where(row >= size, row - size, row)
    column = lax.broadcasted_iota(jnp.int32, (size, size), 1)
    return jnp.where(row == column, 1.0, 0.0).astype(bf16)


def weight_loads(me, mine, other, weights, sems, first):
    core = me & 1
    return [
        pltpu.make_async_copy(
            src.at[i], weights.at[2 * i + (core ^ side)], sems.at[first + 2 * side + i]
        )
        for side, src in enumerate((mine, other))
        for i in range(2)
    ]


def project_kernel(
    at_ref, a0, a1, a2, a3, w0, w1, query_ref, both_ref, rolled_ref, rows, weights, sems
):
    micro_count, group_rows, width = rolled_ref.shape
    tok_rows = group_rows // 4
    wide = query_ref.shape[2]
    block_width = weights.shape[2]
    me = at_ref[0]
    row_copies = [
        pltpu.make_async_copy(src, rows.at[me ^ r], sems.at[r])
        for r, src in enumerate((a0, a1, a2, a3))
    ]
    weight_copies = weight_loads(me, w0, w1, weights, sems, 4)
    for copy in row_copies + weight_copies:
        copy.start()
    for copy in row_copies:
        copy.wait()
    for micro in range(micro_count):
        group = jnp.concatenate(
            [rows[s, micro * tok_rows : (micro + 1) * tok_rows, :] for s in range(4)], axis=0
        )
        turn = roll_matrix(group_rows, at_ref[1 + micro])
        rolled_ref[micro] = dot_wide(turn, group).astype(bf16)
    for copy in weight_copies:
        copy.wait()

    def one(micro, carry):
        own = rows[me, pl.ds(micro * tok_rows, tok_rows), :]
        for block, first, last, offset in spans(0, wide, block_width):
            query_ref[micro, :, offset : offset + last - first] = dot_wide(
                own, weights[block, :, first:last]
            ).astype(bf16)
        group = rolled_ref[micro]
        for block, first, last, offset in spans(wide, 3 * wide, block_width):
            both_ref[micro, :, offset : offset + last - first] = dot_wide(
                group, weights[block, :, first:last]
            ).astype(bf16)
        return carry

    lax.fori_loop(0, micro_count, one, 0)


def project(places, rows, weights, micro_count, wide):
    total_rows, width = rows[0].shape
    tok_rows = total_rows // micro_count
    group_rows = 4 * tok_rows
    block_width = weights[0].shape[2]
    whole = pl.BlockSpec(memory_space=pltpu.VMEM)
    return pl.pallas_call(
        project_kernel,
        in_specs=[pl.BlockSpec(memory_space=pltpu.SMEM)]
        + [pl.BlockSpec(memory_space=pl.ANY)] * 6,
        out_specs=[whole] * 3,
        out_shape=[
            jax.ShapeDtypeStruct((micro_count, tok_rows, wide), bf16),
            jax.ShapeDtypeStruct((micro_count, group_rows, 2 * wide), bf16),
            jax.ShapeDtypeStruct((micro_count, group_rows, width), bf16),
        ],
        scratch_shapes=[
            pltpu.VMEM((4, total_rows, width), bf16),
            pltpu.VMEM((4, width, block_width), bf16),
            pltpu.SemaphoreType.DMA((8,)),
        ],
        compiler_params=pltpu.CompilerParams(vmem_limit_bytes=VMEM_LIMIT),
        cost_estimate=cost(10),
        name="project",
    )(places, *rows, *weights)


def project_back_kernel(
    at_ref,
    query_ref,
    key_ref,
    value_ref,
    rolled_ref,
    own_ref,
    w0,
    w1,
    own_cot_ref,
    group_keep_ref,
    group_give_ref,
    grad_keep_ref,
    grad_give_ref,
    weights,
    stage,
    sems,
):
    micro_count, group_rows, width = rolled_ref.shape
    tok_rows = group_rows // 4
    wide = query_ref.shape[2]
    block_width = weights.shape[2]
    me = at_ref[0]
    weight_copies = weight_loads(me, w0, w1, weights, sems, 0)
    for copy in weight_copies:
        copy.start()
    grad_copies = []
    own_turned = own_ref[...].T
    rolled_turned = rolled_ref[...].reshape(-1, width).T
    for block in range(4):
        low, high = block * block_width, (block + 1) * block_width
        parts = []
        for which, cot_ref in enumerate((query_ref, key_ref, value_ref)):
            first = max(low, which * wide) - which * wide
            last = min(high, (which + 1) * wide) - which * wide
            if first < last:
                left = own_turned if which == 0 else rolled_turned
                right = cot_ref[...].reshape(-1, wide)[:, first:last]
                parts.append(dot_wide(left, right).astype(bf16))
        stage[block] = parts[0] if len(parts) == 1 else jnp.concatenate(parts, axis=1)
        for leaves, target in enumerate((grad_keep_ref, grad_give_ref)):
            copy = pltpu.make_async_copy(
                stage.at[block], target.at[(me ^ block) >> 1], sems.at[4 + block]
            )
            grad_copies.append((((me ^ block) & 1) == leaves, copy))

            @pl.when(((me ^ block) & 1) == leaves)
            def _():
                copy.start()

    for copy in weight_copies:
        copy.wait()

    def one(micro, carry):
        total = None
        for block, first, last, offset in spans(0, wide, block_width):
            part = dot_nt(
                query_ref[micro, :, offset : offset + last - first], weights[block, :, first:last]
            )
            total = part if total is None else total + part
        own_cot_ref[micro] = total
        total = None
        for block, first, last, offset in spans(wide, 3 * wide, block_width):
            source = key_ref if offset < wide else value_ref
            at = offset if offset < wide else offset - wide
            end = at + last - first
            pieces = [(source, at, end, first)]
            if offset < wide < offset + last - first:
                cut = wide - offset
                pieces = [(key_ref, offset, wide, first), (value_ref, 0, end - wide, first + cut)]
            for ref, begin, stop, column in pieces:
                part = dot_nt(
                    ref[micro, :, begin:stop], weights[block, :, column : column + stop - begin]
                )
                total = part if total is None else total + part
        turn = roll_matrix(group_rows, at_ref[1 + micro])
        back = dot_tn(turn, total.astype(bf16)).astype(bf16)
        for s in range(4):
            for leaves, target in enumerate((group_keep_ref, group_give_ref)):

                @pl.when(((me ^ s) & 1) == leaves)
                def _():
                    target[(me ^ s) >> 1, pl.ds(micro * tok_rows, tok_rows), :] = back[
                        s * tok_rows : (s + 1) * tok_rows
                    ]

        return carry

    lax.fori_loop(0, micro_count, one, 0)
    for started, copy in grad_copies:

        @pl.when(started)
        def _():
            copy.wait()


def project_back(places, query_cot, key_cot, value_cot, rolled, own, weights):
    micro_count, group_rows, width = rolled.shape
    tok_rows = group_rows // 4
    block_width = weights[0].shape[2]
    whole = pl.BlockSpec(memory_space=pltpu.VMEM)
    away = pl.BlockSpec(memory_space=pl.ANY)
    return pl.pallas_call(
        project_back_kernel,
        in_specs=[pl.BlockSpec(memory_space=pltpu.SMEM)] + [whole] * 5 + [away] * 2,
        out_specs=[whole, whole, whole, away, away],
        out_shape=[jax.ShapeDtypeStruct((micro_count, tok_rows, width), f32)]
        + [jax.ShapeDtypeStruct((2, micro_count * tok_rows, width), bf16)] * 2
        + [jax.ShapeDtypeStruct((2, width, block_width), bf16)] * 2,
        scratch_shapes=[
            pltpu.VMEM((4, width, block_width), bf16),
            pltpu.VMEM((4, width, block_width), bf16),
            pltpu.SemaphoreType.DMA((8,)),
        ],
        compiler_params=pltpu.CompilerParams(vmem_limit_bytes=VMEM_LIMIT),
        cost_estimate=cost(14),
        name="project_back",
    )(places, query_cot, key_cot, value_cot, rolled, own, *weights)


CHUNKS = 8


def dense_kernel(
    att_ref,
    start_ref,
    cot_ref,
    gain_ref,
    place_ref,
    big_ref,
    out_ref,
    mid_cot_ref,
    att_cot_ref,
    gain_cot_ref,
    grad_ref,
    up_v,
    down_v,
    output_v,
    mid_v,
    normed_v,
    inv_v,
    ffn_v,
    branch_v,
    total_v,
    back_v,
    up_s,
    cot_s,
    gelu_v,
    cot_v,
    up_stage,
    down_stage,
    output_stage,
    zero_v,
    sems,
    grad_sems,
):
    rows, width = start_ref.shape
    own = width // CHUNKS
    third = own // 3
    pair = CHUNKS // 4
    step = rows // 3
    output_copy = pltpu.make_async_copy(
        big_ref.at[:, pl.ds(0, 3), pl.ds(2 * own, third)], output_v, sems.at[8]
    )

    def up_copy(j):
        return pltpu.make_async_copy(big_ref.at[:, j, pl.ds(0, own)], up_v.at[j], sems.at[j])

    def down_copy(j):
        return pltpu.make_async_copy(
            big_ref.at[pl.ds(j * pair, pair), :, pl.ds(own, own)], down_v.at[j], sems.at[4 + j]
        )

    def up_out(j):
        return pltpu.make_async_copy(
            up_stage.at[j], grad_ref.at[:, j, pl.ds(0, own)], grad_sems.at[j]
        )

    def down_out(j):
        return pltpu.make_async_copy(
            down_stage.at[j],
            grad_ref.at[pl.ds(j * pair, pair), :, pl.ds(own, own)],
            grad_sems.at[4 + j],
        )

    output_copy.start()
    for j in range(4):
        up_copy(j).start()
        down_copy(j).start()
    zero_v[...] = jnp.zeros_like(zero_v)
    zero_copy = pltpu.make_async_copy(
        zero_v, grad_ref.at[:, 3, pl.ds(2 * own, third)], grad_sems.at[8]
    )
    zero_copy.start()
    att = dot_nt(att_ref[...], place_ref[...]).astype(bf16)
    branch_v[...] = cot_ref[...].astype(bf16)
    output_copy.wait()
    output_w = output_v[...].reshape(width, width)
    gain = gain_ref[...]
    mid_v[...] = start_ref[...] + dot_wide(att, output_w)
    for part in range(3):
        at = slice(part * step, (part + 1) * step)
        mid = mid_v[at]
        centre = mid - jnp.mean(mid, axis=1, keepdims=True)
        inv_std = lax.rsqrt(jnp.mean(centre * centre, axis=1, keepdims=True) + NORM_EPS)
        normed = centre * inv_std
        normed_v[at] = normed
        inv_v[at] = jnp.broadcast_to(inv_std, (step, LANES))
        ffn_v[at] = (normed * gain).astype(bf16)
    ffn_turned = ffn_v[...].T
    total_v[...] = mid_v[...]
    back_v[...] = jnp.zeros_like(back_v)

    def one(j, carry):
        up_copy(j).wait()
        down_copy(j).wait()
        up_w = up_v[j].reshape(width, width)
        down_w = down_v[j].reshape(width, width)
        up_s[...] = dot_wide(ffn_v[...], up_w)
        cot_s[...] = dot_nt(branch_v[...], down_w)
        gelus, cots = [], []
        for start in range(0, rows, 64):
            at = slice(start, start + 64)
            up = up_s[at]
            square = up * up
            root = math.sqrt(2.0 / math.pi)
            bend = jnp.tanh(up * (root + (root * 0.044715) * square))
            half = 0.5 + 0.5 * bend
            slope = half + up * (0.5 - 0.5 * bend * bend) * (
                root + (root * 3 * 0.044715) * square
            )
            gelus.append((up * half).astype(bf16))
            cots.append((cot_s[at] * slope).astype(bf16))
        gelu = jnp.concatenate(gelus, axis=0)
        cot = jnp.concatenate(cots, axis=0)
        gelu_v[...] = gelu
        cot_v[...] = cot
        total_v[...] += dot_wide(gelu_v[...], down_w)
        back_v[...] += dot_nt(cot_v[...], up_w)
        up_stage[j] = dot_wide(ffn_turned, cot_v[...]).astype(bf16).reshape(up_stage.shape[1:])
        up_out(j).start()
        down_stage[j] = (
            dot_tn(gelu_v[...], branch_v[...]).astype(bf16).reshape(down_stage.shape[1:])
        )
        down_out(j).start()
        return carry

    lax.fori_loop(0, 4, one, 0)
    out_ref[...] = total_v[...].astype(bf16)
    gain_cot = jnp.zeros((1, width), f32)
    for part in range(3):
        at = slice(part * step, (part + 1) * step)
        back = back_v[at]
        normed = normed_v[at]
        gain_cot = gain_cot + jnp.sum(back * normed, axis=0, keepdims=True)
        scaled = back * gain
        mid_cot = cot_ref[at] + inv_v[at][:, :1] * (
            scaled
            - jnp.mean(scaled, axis=1, keepdims=True)
            - normed * jnp.mean(scaled * normed, axis=1, keepdims=True)
        )
        mid_cot_ref[at] = mid_cot
        cot_v[at] = mid_cot.astype(bf16)
    gain_cot_ref[...] = gain_cot
    att_cot = dot_nt(cot_v[...], output_w).astype(bf16)
    att_cot_ref[...] = dot_wide(att_cot, place_ref[...]).astype(bf16)
    output_stage[...] = dot_tn(att, cot_v[...]).astype(bf16).reshape(output_stage.shape)
    output_out = pltpu.make_async_copy(
        output_stage, grad_ref.at[:, pl.ds(0, 3), pl.ds(2 * own, third)], grad_sems.at[9]
    )
    output_out.start()
    for j in range(4):
        up_out(j).wait()
        down_out(j).wait()
    output_out.wait()
    zero_copy.wait()


def dense(attended, start, out_cot, gain, place_heads, big):
    rows, width = start.shape
    wide = attended.shape[1]
    own = width // CHUNKS
    third = own // 3
    pair = CHUNKS // 4
    whole = pl.BlockSpec(memory_space=pltpu.VMEM)
    away = pl.BlockSpec(memory_space=pl.ANY)
    return pl.pallas_call(
        dense_kernel,
        in_specs=[whole] * 5 + [away],
        out_specs=[whole] * 4 + [away],
        out_shape=[
            jax.ShapeDtypeStruct((rows, width), bf16),
            jax.ShapeDtypeStruct((rows, width), f32),
            jax.ShapeDtypeStruct((rows, wide), bf16),
            jax.ShapeDtypeStruct((1, width), f32),
            jax.ShapeDtypeStruct(big.shape, bf16),
        ],
        scratch_shapes=[
            pltpu.VMEM((4, CHUNKS, own, width), bf16),
            pltpu.VMEM((4, pair, 4, own, width), bf16),
            pltpu.VMEM((CHUNKS, 3, third, width), bf16),
            pltpu.VMEM((rows, width), f32),
            pltpu.VMEM((rows, width), f32),
            pltpu.VMEM((rows, LANES), f32),
            pltpu.VMEM((rows, width), bf16),
            pltpu.VMEM((rows, width), bf16),
            pltpu.VMEM((rows, width), f32),
            pltpu.VMEM((rows, width), f32),
            pltpu.VMEM((rows, width), f32),
            pltpu.VMEM((rows, width), f32),
            pltpu.VMEM((rows, width), bf16),
            pltpu.VMEM((rows, width), bf16),
            pltpu.VMEM((4, CHUNKS, own, width), bf16),
            pltpu.VMEM((4, pair, 4, own, width), bf16),
            pltpu.VMEM((CHUNKS, 3, third, width), bf16),
            pltpu.VMEM((CHUNKS, third, width), bf16),
            pltpu.SemaphoreType.DMA((9,)),
            pltpu.SemaphoreType.DMA((10,)),
        ],
        compiler_params=pltpu.CompilerParams(vmem_limit_bytes=VMEM_LIMIT),
        cost_estimate=cost(25),
        name="dense",
    )(attended, start, out_cot, gain, place_heads, big)


def place_matrix(source, piece, padded):
    index = jnp.arange(source, dtype=jnp.int32)
    target = (index // piece) * padded + index % piece
    spots = jnp.arange(source // piece * padded, dtype=jnp.int32)
    return (target[:, None] == spots[None, :]).astype(bf16)


def dot_low(left, right):
    return jnp.dot(left, right, preferred_element_type=f32).astype(bf16)


def roll_rows(value, shift, axis):
    size = value.shape[axis]
    twice = jnp.concatenate([value, value], axis=axis)
    return lax.dynamic_slice_in_dim(twice, shift, size, axis)


def gather_shards(shard):
    return lax.all_gather(shard, "fsdp", axis=0, tiled=True)


def reduce_shards(grad):
    part = lax.psum_scatter(grad, "fsdp", scatter_dimension=0, tiled=True)
    return lax.psum(part.astype(bf16), "seq").astype(f32)[0]


LINE = 4


def place():
    fsdp_index, seq_index = lax.axis_index("fsdp"), lax.axis_index("seq")
    return fsdp_index // 2, fsdp_index % 2, seq_index // 2, seq_index % 2


def flip(value, axis, bit):
    return lax.ppermute(value, axis, [(i, i ^ bit) for i in range(lax.axis_size(axis))])


def along_line(value, step):
    pairs = [
        (z * 2 + y, (z + step) % LINE * 2 + y) for z in range(LINE) for y in range(2)
    ]
    return lax.ppermute(value, "fsdp", pairs)


def line_gather(block, axis=0):
    z = place()[0]
    parts = [block] + [along_line(block, step) for step in range(1, LINE)]
    ring = jnp.stack([parts[-step % LINE] for step in range(LINE)] * 2, axis=axis)
    return lax.dynamic_slice_in_dim(ring, (LINE - z) % LINE, LINE, axis)


def in_line(parts, axis=0):
    z = place()[0]
    return jnp.stack(
        [lax.select_n((z + LINE - at) % LINE, *parts) for at in range(LINE)], axis=axis
    )


def pair_gather(value, bit_axis, bit, own_bit, axis=0):
    other = flip(value, bit_axis, bit)
    return jnp.stack(
        [jnp.where(own_bit == 0, value, other), jnp.where(own_bit == 0, other, value)], axis=axis
    )


def pair_reduce(value, bit_axis, bit, own_bit, axis=0):
    keep, give = pair_split(value, own_bit, axis)
    return add_low(keep, flip(give, bit_axis, bit))


def pair_split(value, own_bit, axis):
    keep = lax.dynamic_index_in_dim(value, own_bit, axis, keepdims=False)
    return keep, lax.dynamic_index_in_dim(value, 1 - own_bit, axis, keepdims=False)


def add_low(left, right):
    return (left.astype(f32) + right.astype(f32)).astype(left.dtype)


def line_reduce(value, *others):
    z = place()[0]
    total = lax.dynamic_index_in_dim(value, z, 0, keepdims=False).astype(f32)
    for step in range(1, LINE):
        give = lax.dynamic_index_in_dim(value, (z + step) % LINE, 0, keepdims=False)
        total = total + after(along_line(give, step), *others).astype(f32)
    return total


def fast_mesh():
    return (lax.axis_size("fsdp"), lax.axis_size("seq")) == (2 * LINE, 4)


def exact_parts(value):
    parts = []
    for _ in range(2):
        part = lax.reduce_precision(value, 8, 7)
        parts.append(part.astype(bf16))
        value = value - part
    return parts + [value.astype(bf16)]


def gather_small(small, stamps):
    if not fast_mesh():
        whole = lax.all_gather(small, "fsdp", axis=0)
        return whole, lax.all_gather(stamps, "fsdp", axis=0), whole
    parts = jnp.concatenate(exact_parts(stamps))
    row = jnp.pad(parts, (0, LANES - parts.shape[0]))[None]
    packed = jnp.concatenate([small, jnp.pad(row, ((0, 15), (0, 0)))], axis=0)
    line = line_gather(packed)
    packed = pair_gather(line, "fsdp", 1, place()[1], 1)
    packed = packed.reshape((2 * LINE,) + packed.shape[2:])
    count = stamps.shape[0]
    row = packed[:, small.shape[0]].astype(f32)
    stamps_all = row[:, :count] + row[:, count : 2 * count] + row[:, 2 * count : 3 * count]
    return packed[:, : small.shape[0]], stamps_all, line


def after(value, *others):
    if not others:
        return value
    return lax.optimization_barrier((value,) + others)[0]


def scatter_groups(value):
    if not fast_mesh():
        return lax.psum_scatter(value, "fsdp", scatter_dimension=0, tiled=True)[0], value
    y, core = place()[1], place()[3]
    half = value.shape[2] // 2
    value = lax.dynamic_slice_in_dim(value, core * half, half, 2)
    value = value.reshape((LINE, 2) + value.shape[1:])
    first = pair_reduce(value, "fsdp", 1, y, 1)
    value = line_reduce(first)
    other = flip(value, "seq", 1)
    value = jnp.concatenate(
        [jnp.where(core == 0, value, other), jnp.where(core == 0, other, value)], axis=1
    )
    return value, first


def gather_big(output_weight, up_weight, down_weight, *others):
    if not fast_mesh():
        up, down, output = (gather_shards(w) for w in (up_weight, down_weight, output_weight))
        width = output.shape[0]
        own = width // CHUNKS
        return join_big(
            up.reshape(CHUNKS, own, 4, width).transpose(0, 2, 1, 3),
            down.reshape(CHUNKS, 4, own, width),
            output.reshape(CHUNKS, own, width),
        )
    seq_index = lax.axis_index("seq")
    own, width = output_weight.shape
    third = own // 3
    quarter = jnp.concatenate(
        [
            lax.dynamic_slice_in_dim(up_weight, seq_index * width, width, 1),
            lax.dynamic_slice_in_dim(down_weight, seq_index * own, own, 0),
            lax.dynamic_slice_in_dim(
                jnp.pad(output_weight, ((0, third), (0, 0))), seq_index * third, third, 0
            ),
        ],
        axis=0,
    )
    big = lax.all_gather(after(quarter, *others), ("fsdp", "seq"), axis=0)
    return big.reshape((CHUNKS, 4) + quarter.shape)


def join_big(up, down, output):
    chunks, own, width = output.shape
    third = own // 3
    output = jnp.pad(output, ((0, 0), (0, third), (0, 0))).reshape(chunks, 4, third, width)
    return jnp.concatenate([up, down, output], axis=2)


def reduce_big(grad):
    chunks, quarters, rows, width = grad.shape
    own = width // CHUNKS
    if not fast_mesh():
        fsdp_count = lax.axis_size("fsdp")
        up = grad[:, :, :own].transpose(0, 2, 1, 3).reshape(fsdp_count, -1, 4 * width)
        down = grad[:, :, own : 2 * own].reshape(fsdp_count, -1, width)
        output = grad[:, :3, 2 * own :].reshape(fsdp_count, -1, width)
        return tuple(reduce_shards(g) for g in (up, down, output))
    total = lax.psum_scatter(
        grad.reshape(chunks * quarters, rows, width),
        ("fsdp", "seq"),
        scatter_dimension=0,
        tiled=True,
    )
    return total[0]


def four_ways(value):
    return value, flip(value, "seq", 1), flip(value, "seq", 2)


def fourth(three, *others):
    if not fast_mesh():
        return three
    value, near, across = three
    across = after(across, *others)
    return value, near, across, flip(across, "seq", 1)


def gather_projections(weight):
    columns = weight.shape[1] // 4
    if not fast_mesh():
        full = gather_shards(weight)
        blocks = [full[:, i * columns : (i + 1) * columns] for i in range(4)]
        return (jnp.stack(blocks[::2]), jnp.stack(blocks[1::2])), weight
    y, core = place()[1], place()[3]
    pair = jnp.stack(
        [
            lax.dynamic_slice_in_dim(weight, (core + 2 * i) * columns, columns, 1)
            for i in range(2)
        ]
    )
    line = line_gather(pair, 1)
    return (line, flip(line, "fsdp", 1)), line


def finish_projections(pair, *others):
    if not fast_mesh():
        return pair
    y = place()[1]
    line, other = pair
    other = after(other, *others)
    pair = jnp.stack(
        [jnp.where(y == 0, line, other), jnp.where(y == 0, other, line)], axis=2
    ).reshape(2, -1, line.shape[-1])
    return pair, flip(pair, "seq", 1)


def gather_group(value):
    if not fast_mesh():
        rows = lax.all_gather(value, "seq", axis=0)
        return tuple(rows[i] for i in range(4))
    return four_ways(value)


def in_order(keep, give):
    return keep[0], give[0], keep[1], give[1]


def reduce_group(keep, give):
    order = jnp.stack(in_order(keep, give))
    return lax.psum_scatter(order, "seq", scatter_dimension=0, tiled=True)[0].astype(f32)


def reduce_projections(keep, give):
    order = jnp.concatenate(in_order(keep, give), axis=1)
    return reduce_shards(order.reshape(lax.axis_size("fsdp"), -1, order.shape[1]))


def gather_finals(value, *others):
    x, core = place()[2:]
    width = value.shape[1]
    own = width // CHUNKS
    other = after(flip(value, "seq", 2), *others)
    total = jnp.stack([jnp.where(x == 0, value, other), jnp.where(x == 0, other, value)])
    total = pair_gather(total, "seq", 1, core, 1).astype(f32)
    total = total.reshape((4,) + value.shape)
    return (
        total[:, :own].transpose(1, 0, 2).reshape(own, -1),
        total[:, own : 2 * own].transpose(1, 0, 2).reshape(own, -1),
        total[:, 2 * own : 3 * own].reshape(-1, width),
        total[:3, 3 * own :].reshape(own, width),
    )


def join_lanes(value, lanes):
    return jnp.concatenate(
        [value[:, at : at + lanes] for at in range(0, value.shape[1], lanes)], axis=0
    )


def line_exchange(give, times, *others):
    z = place()[0]
    rows = give.shape[1]
    total = lax.dynamic_index_in_dim(give, z, 0, keepdims=False).astype(f32)
    parts = [times]
    for step in range(1, LINE):
        piece = lax.dynamic_index_in_dim(give, (z + step) % LINE, 0, keepdims=False)
        other = after(along_line(jnp.concatenate([piece, times], axis=0), step), *others)
        total = total + other[:rows].astype(f32)
        parts.append(other[rows:])
    return total, in_line(parts)


def pair_exchange(grad, times):
    y = place()[1]
    rows, lanes = grad.shape[2:]
    keep = lax.dynamic_index_in_dim(grad, y, 1, keepdims=False)
    give = lax.dynamic_index_in_dim(grad, 1 - y, 1, keepdims=False)
    give = jnp.concatenate([give.reshape(LINE * rows, lanes), times], axis=0)
    other = flip(give, "fsdp", 1)
    keep = add_low(keep, other[: LINE * rows].reshape(keep.shape))
    late = other[LINE * rows :]
    times = jnp.concatenate(
        [jnp.where(y == 0, times, late), jnp.where(y == 0, late, times)], axis=0
    )
    return keep, times


def body(
    hidden_in,
    row_types,
    lengths,
    noise_time,
    coords,
    residue_table,
    atom_table,
    time_weight,
    first_gain,
    query_weight,
    key_weight,
    value_weight,
    output_weight,
    kernel_mean,
    kernel_width,
    pair_weight,
    second_gain,
    up_weight,
    down_weight,
    force_weight,
    layer_cot,
    force_cot,
):
    seq_count = lax.axis_size("seq")
    fsdp_count = lax.axis_size("fsdp")
    seq_index = lax.axis_index("seq")
    micro_count, tok_rows, model_width = hidden_in.shape
    group_rows = tok_rows * seq_count
    own_kernels, head_count = pair_weight.shape
    kernels = own_kernels * fsdp_count
    head_dim = model_width // head_count
    inv_root = head_dim ** (-0.5)
    wide_heads = head_count * HEAD_PAD
    total_rows = micro_count * tok_rows
    residues, own_width = residue_table.shape
    types = residues + atom_table.shape[0]
    offset = seq_index * tok_rows

    small_rows = types + 16
    small = jnp.concatenate(
        [
            residue_table,
            atom_table,
            force_weight,
            first_gain[None],
            second_gain[None],
            jnp.zeros((small_rows - types - 5, own_width), bf16),
        ],
        axis=0,
    )
    small = jnp.pad(small, ((0, 0), (0, LANES - own_width)))
    kernel_rows = jnp.concatenate([pair_weight, kernel_mean[:, None], kernel_width[:, None]], axis=1)
    kernel_rows = jnp.pad(kernel_rows, ((0, 0), (0, LANES - head_count - 2)))
    big = gather_big(output_weight, up_weight, down_weight)
    small_all, stamps_all, small_line = gather_small(
        jnp.concatenate([small, kernel_rows], axis=0), noise_time[:, 0].reshape(-1)
    )
    head_place = place_matrix(model_width, head_dim, HEAD_PAD)
    qkv_weight = jnp.concatenate(
        [dot_low(w, head_place) for w in (query_weight, key_weight, value_weight)], axis=1
    )
    qkv_blocks, qkv_line = gather_projections(qkv_weight)
    kernel_all = small_all[:, small_rows:].reshape(kernels, LANES)
    pair_full = kernel_all[:, :head_count].astype(f32)
    mean_full = kernel_all[:, head_count].astype(f32)
    width_full = kernel_all[:, head_count + 1].astype(f32)
    spread = place_matrix(model_width, own_width, LANES)
    tables = dot_low(
        small_all[:, :small_rows].transpose(1, 0, 2).reshape(small_rows, fsdp_count * LANES),
        spread.T,
    )
    type_table = tables[:types]
    force_wide = tables[types : types + 3].astype(f32)
    gain_one = tables[types + 3].astype(f32)
    gain_two = tables[types + 4].astype(f32)

    coords = after(coords, small_line)
    doc_lengths = lengths[:, 0]
    documents = jnp.arange(doc_lengths.shape[1], dtype=jnp.int32)
    earlier = documents[:, None] <= documents[None, :]
    bounds = jnp.sum(jnp.where(earlier[None], doc_lengths[:, :, None], 0), axis=1)
    first_len = doc_lengths[:, 0]
    all_rows = jnp.arange(group_rows, dtype=jnp.int32)
    key_doc = jnp.sum((all_rows[None, :, None] >= bounds[:, None, :]).astype(jnp.int32), axis=2)
    query_doc = lax.dynamic_slice_in_dim(key_doc, offset, tok_rows, 1)
    query_pos = lax.dynamic_slice_in_dim(coords, offset, tok_rows, 2)
    roll_index = (all_rows[None, :] + first_len[:, None]) % group_rows
    rolled_doc = jnp.sum(
        (roll_index[:, :, None] >= bounds[:, None, :]).astype(jnp.int32), axis=2
    )
    rolled_pos = jnp.stack([roll_rows(coords[m], first_len[m], 1) for m in range(micro_count)])
    same_doc = query_doc[:, :, None] == rolled_doc[:, None, :]
    mask = jnp.where(same_doc, 0.0, -1e30).astype(f32)
    delta = query_pos[:, :, :, None] - rolled_pos[:, :, None, :]
    dist = jnp.sqrt(jnp.sum(delta * delta, axis=1))
    long_row = (query_doc == 1).reshape(micro_count, tok_rows // TILE_ROWS, TILE_ROWS)
    flags = jnp.where(
        jnp.all(long_row, axis=2), 0, jnp.where(jnp.any(long_row, axis=2), 2, 1)
    ).astype(jnp.int32)

    scale_k = 1.0 / (math.sqrt(2.0 * math.pi) * width_full)
    coef = (-0.5 * LOG2E) / (width_full * width_full)
    mean_wide = jnp.broadcast_to(mean_full[:, None], (kernels, LANES))
    coef_wide = jnp.broadcast_to(coef[:, None], (kernels, LANES))
    base_wide = jnp.broadcast_to(jnp.log2(scale_k)[:, None], (kernels, LANES))
    bias_weight = pair_full.T.astype(bf16)
    bias_args = (mask, mean_wide, coef_wide, base_wide, bias_weight)

    doc_hot = (
        query_doc[:, :, None] == jnp.arange(doc_lengths.shape[1], dtype=jnp.int32)
    ).astype(f32)
    type_hot = (
        row_types.reshape(total_rows)[:, None] == jnp.arange(types, dtype=jnp.int32)
    ).astype(bf16)
    time_low = sinus_columns(
        stamps_all, model_width, lax.axis_index("fsdp") * own_width, own_width
    )
    time_proj = dot_wide(time_low.reshape(-1, own_width), time_weight)
    time_proj, time_step = scatter_groups(time_proj.reshape(fsdp_count, -1, model_width))
    bias = pair_bias(0, None, flags, dist, *bias_args)
    bias = pair_bias(1, bias, flags, after(dist, qkv_line, time_step), *bias_args)
    time_proj = time_proj.reshape(micro_count, -1, model_width)
    start_state = (
        hidden_in.astype(f32)
        + dot_wide(type_hot, type_table).reshape(hidden_in.shape)
        + jnp.einsum("min,mnd->mid", doc_hot, time_proj, precision=EXACT)
    ).reshape(total_rows, model_width)
    normed_in, normed_one, inv_one = norm_forward(start_state, gain_one)
    attn_in = normed_in.astype(bf16)

    four = seq_index if fast_mesh() else 0
    places = jnp.concatenate([jnp.full((1,), four, jnp.int32), first_len])
    attn_rows = gather_group(attn_in)
    for micro in range(2, micro_count):
        bias = pair_bias(micro, bias, flags, after(dist, attn_in), *bias_args)
    attn_rows = fourth(attn_rows, bias)
    qkv_blocks = finish_projections(qkv_blocks, bias)
    queries, both, rolled = project(places, attn_rows, qkv_blocks, micro_count, wide_heads)
    probs, attended = attend(queries, both, bias, inv_root * LOG2E)
    forces_cot = force_cot.transpose(1, 0, 2).reshape(3, total_rows)
    out_grad = layer_cot.reshape(total_rows, model_width).astype(f32)
    for axis in range(3):
        out_grad = out_grad + forces_cot[axis][:, None] * force_wide[axis][None, :]
    layer_out, mid_grad, attended_grad, gain_two_grad, big_grad = dense(
        attended.reshape(total_rows, wide_heads),
        start_state,
        out_grad,
        gain_two[None],
        head_place,
        big,
    )
    big_sum = reduce_big(big_grad)
    forces = dot_nt(force_wide.astype(bf16), layer_out)
    forces = forces.reshape(3, micro_count, tok_rows).transpose(1, 0, 2)
    force_w_grad = jnp.dot(forces_cot, layer_out.astype(f32), precision=EXACT)

    score_cot, query_low, key_part, value_part = attend_back(
        queries,
        both,
        attended_grad.reshape(micro_count, tok_rows, wide_heads),
        probs,
        inv_root,
    )
    own_part, group_keep, group_give, qkv_keep, qkv_give = project_back(
        places, query_low, key_part, value_part, rolled, attn_in, qkv_blocks
    )

    def pair_sums(micro, earlier, *others):
        part = pair_grads(
            micro, flags, after(dist, earlier, *others), score_cot, mean_wide, coef_wide
        )
        return part if micro == 0 else earlier + part

    sums = pair_sums(0, group_give)
    if fast_mesh():
        group_other, qkv_other = (flip(v, "seq", 1) for v in (group_give, qkv_give))
        group_near = add_low(group_keep, after(group_other, sums))
        qkv_near = add_low(qkv_keep, after(qkv_other, sums))
        qkv_near = qkv_near.reshape((2, LINE, 2, -1) + qkv_near.shape[2:])
        pair_keep, pair_give = pair_split(qkv_near, place()[1], 2)
        group_other = flip(group_near[1], "seq", 2)
        qkv_other = flip(pair_give, "fsdp", 1)
        sums = pair_sums(1, sums, group_near, pair_give)
        group_sum = group_near[0].astype(f32) + after(group_other, sums).astype(f32)
    else:
        group_sum = reduce_group(group_keep, group_give)
    attn_in_grad = own_part.reshape(total_rows, model_width) + group_sum
    norm_part_one, gain_one_grad = norm_backward(attn_in_grad, normed_one, inv_one, gain_one)
    input_grad = mid_grad + norm_part_one

    input_low = input_grad.astype(bf16)
    type_grad = dot_tn(type_hot, input_low)
    time_cot = jnp.einsum(
        "min,mid->mnd",
        doc_hot.astype(bf16),
        input_low.reshape(micro_count, tok_rows, model_width),
        preferred_element_type=f32,
    ).reshape(-1, model_width)
    small_grad = jnp.concatenate(
        [
            type_grad,
            force_w_grad,
            gain_one_grad[None],
            gain_two_grad,
            jnp.zeros((small_rows - types - 5, model_width), f32),
        ],
        axis=0,
    )
    small_grad = dot_low(small_grad.astype(bf16), spread)
    small_grad = small_grad.reshape(small_rows, fsdp_count, LANES).transpose(1, 0, 2)

    def kernel_grads(sums):
        plain, once, once_low, twice, twice_low = (
            sums[k * head_count : (k + 1) * head_count].T for k in range(5)
        )
        centre = (mean_full - CENTRE)[:, None]
        once = once + once_low
        twice = twice + twice_low - centre * (2.0 * once - centre * plain)
        once = once - centre * plain
        pair_w_grad = plain * scale_k[:, None]
        inv_width = 1.0 / width_full
        mean_grad = jnp.sum(pair_full * once, axis=1) * scale_k * inv_width * inv_width
        width_grad = (
            jnp.sum(pair_full * (twice * (inv_width * inv_width)[:, None] - plain), axis=1)
            * scale_k
            * inv_width
        )
        grad = jnp.concatenate(
            [pair_w_grad, mean_grad[:, None], width_grad[:, None]], axis=1
        ).astype(bf16)
        grad = jnp.pad(grad, ((0, 0), (0, LANES - head_count - 2)))
        return grad.reshape(fsdp_count, own_kernels, LANES)

    if fast_mesh():
        small_other, time_other = (flip(v, "seq", 1) for v in (small_grad, time_cot))
        qkv_pair = add_low(pair_keep, after(qkv_other, small_grad, time_cot))
        qkv_other = flip(qkv_pair[1], "seq", 2)
        small_one, time_one = small_grad + small_other, time_cot + time_other
        for micro in range(2, micro_count):
            sums = pair_sums(micro, sums, qkv_pair, small_one, time_one)
        small_other, time_other = (flip(v, "seq", 2) for v in (small_one, time_one))
        qkv_far = add_low(qkv_pair[0], after(qkv_other, sums))
        kernel_grad = kernel_grads(after(sums, qkv_far))
        for bit in (1, 2):
            kernel_grad = kernel_grad + flip(kernel_grad, "seq", bit)
        small_two = small_one + after(small_other, sums)
        time_two = time_one + after(time_other, sums)
        small_two = jnp.concatenate([small_two, kernel_grad], axis=1)
        small_two = small_two.reshape((LINE, 2) + small_two.shape[1:])
        time_two = join_lanes(time_two.astype(bf16), LANES)
        small_half, time_pair = pair_exchange(small_two, time_two)
        qkv_own = line_reduce(qkv_far, small_half, time_pair).astype(bf16)
        finals = jnp.concatenate([qkv_own, big_sum], axis=0)
        small_sum, time_cots = line_exchange(small_half, time_pair, finals)
        time_cots = time_cots.reshape(
            fsdp_count, model_width // LANES, -1, LANES
        ).transpose(0, 2, 1, 3)
    else:
        for micro in range(1, micro_count):
            sums = pair_sums(micro, sums)
        small_sum = reduce_shards(jnp.concatenate([small_grad, kernel_grads(sums)], axis=1))
        time_cots = lax.all_gather(lax.psum(time_cot, "seq").astype(bf16), "fsdp", axis=0)
        finals = (reduce_projections(qkv_keep, qkv_give),) + big_sum
    row_sum = small_sum[:small_rows, :own_width]
    kernel_sum = small_sum[small_rows:]
    time_sum = dot_tn(time_low.reshape(-1, own_width), time_cots.reshape(-1, model_width))
    if fast_mesh():
        finals = gather_finals(finals, small_sum, time_cots)
    qkv_sum, up_sum, down_sum, output_sum = finals
    qkv_low = join_lanes(qkv_sum.astype(bf16), wide_heads)
    query_sum, key_sum, value_sum = dot_nt(qkv_low, head_place).reshape(3, -1, model_width)
    return (
        layer_out.reshape(hidden_in.shape),
        forces,
        input_grad.reshape(hidden_in.shape),
        row_sum[:residues],
        row_sum[residues:types],
        time_sum,
        row_sum[types + 3],
        query_sum,
        key_sum,
        value_sum,
        output_sum,
        kernel_sum[:, head_count],
        kernel_sum[:, head_count + 1],
        kernel_sum[:, :head_count],
        row_sum[types + 4],
        up_sum,
        down_sum,
        row_sum[types : types + 3],
    )


def solution(mesh):
    rows = ("fsdp", "seq")
    return jax.shard_map(
        body,
        mesh=mesh,
        in_specs=(
            P(None, rows, None),
            P(None, rows),
            P(None, "fsdp", None),
            P(None, "fsdp", None),
            P(None, None, "fsdp"),
            P(None, "fsdp"),
            P(None, "fsdp"),
            P("fsdp", None),
            P("fsdp"),
            P("fsdp", None),
            P("fsdp", None),
            P("fsdp", None),
            P("fsdp", None),
            P("fsdp"),
            P("fsdp"),
            P("fsdp", None),
            P("fsdp"),
            P("fsdp", None),
            P("fsdp", None),
            P(None, "fsdp"),
            P(None, rows, None),
            P(None, None, rows),
        ),
        out_specs=(
            P(None, rows, None),
            P(None, None, rows),
            P(None, rows, None),
            P(None, "fsdp"),
            P(None, "fsdp"),
            P("fsdp", None),
            P("fsdp"),
            P("fsdp", None),
            P("fsdp", None),
            P("fsdp", None),
            P("fsdp", None),
            P("fsdp"),
            P("fsdp"),
            P("fsdp", None),
            P("fsdp"),
            P("fsdp", None),
            P("fsdp", None),
            P(None, "fsdp"),
        ),
        check_vma=False,
    )
```

```python
import functools
import math

import jax
import jax.numpy as jnp
from jax import lax
from jax.experimental import pallas as pl
from jax.experimental.pallas import tpu as pltpu
from jax.sharding import PartitionSpec as P

NORM_EPS = 1e-05
PROTEIN_ROWS = 384
LANES = 128
HEAD_PAD = 32
TILE_ROWS = 8
ROW_BLOCK = 32
CENTRE = 6.0
PER_STEP = 4
LOG2E = math.log2(math.e)
VMEM_LIMIT = 56 * 2**20
EXACT = lax.Precision.HIGHEST
bf16 = jnp.bfloat16
f32 = jnp.float32


def dot_wide(left, right):
    return jnp.dot(left, right, preferred_element_type=f32)


def dot_tn(left, right):
    return lax.dot_general(left, right, (((0,), (0,)), ((), ())), preferred_element_type=f32)


def dot_nt(left, right):
    return lax.dot_general(left, right, (((1,), (1,)), ((), ())), preferred_element_type=f32)


def cost(micros):
    return pl.CostEstimate(flops=int(micros * 0.04e9), bytes_accessed=0, transcendentals=0)


def sinus_columns(stamps, model_width, first, columns):
    half_width = model_width // 2
    index = first + jnp.arange(columns, dtype=jnp.int32)
    step = (index % half_width).astype(f32)
    frequency = jnp.exp(-math.log(10000.0) * step / half_width)
    angles = 1000.0 * stamps[..., None] * frequency
    return jnp.where(index < half_width, jnp.sin(angles), jnp.cos(angles)).astype(bf16)


def norm_forward(value, norm_gain):
    centre = value - jnp.mean(value, axis=-1, keepdims=True)
    inv_std = lax.rsqrt(jnp.mean(centre * centre, axis=-1, keepdims=True) + NORM_EPS)
    normed = centre * inv_std
    return normed * norm_gain, normed, inv_std


def norm_backward(grad_out, normed, inv_std, norm_gain):
    scaled = grad_out * norm_gain
    grad_in = inv_std * (
        scaled
        - jnp.mean(scaled, axis=-1, keepdims=True)
        - normed * jnp.mean(scaled * normed, axis=-1, keepdims=True)
    )
    return grad_in, jnp.sum(grad_out * normed, axis=0)


def density_rows(spans, mean_ref, coef_ref, base_ref):
    kernels = mean_ref.shape[0]
    tiles = spans[0].shape[1] // LANES
    parts = []
    for start in range(0, kernels, 16):
        mean = mean_ref[start : start + 16, :]
        coef = coef_ref[start : start + 16, :]
        pieces = []
        for span in spans:
            for tile in range(tiles):
                shift = span[:, tile * LANES : (tile + 1) * LANES] - mean
                power = shift * shift * coef
                if base_ref is not None:
                    power = power + base_ref[start : start + 16, :]
                pieces.append(jnp.exp2(power).astype(bf16))
        parts.append(jnp.concatenate(pieces, axis=1))
    return jnp.concatenate(parts, axis=0)


def bias_kernel(
    micro, flag_ref, dist_ref, mask_ref, mean_ref, coef_ref, base_ref, weight_ref, *rest
):
    out_ref = rest[-1]
    row_count, columns = dist_ref.shape
    heads = weight_ref.shape[0]
    long_tiles = PROTEIN_ROWS // LANES
    all_tiles = columns // LANES

    def fill(base, first, tiles):
        empty = jnp.full((TILE_ROWS, LANES), -1e30, f32)
        for tile in range(first, first + tiles):
            for head in range(heads):
                out_ref[tile, pl.ds(head * row_count + base, TILE_ROWS), :] = empty

    def compute(base, first, tiles, batch):
        span = slice(first * LANES, (first + tiles) * LANES)
        dist = dist_ref[pl.ds(base, TILE_ROWS), span]
        mask = mask_ref[pl.ds(base, TILE_ROWS), span]
        for start in range(0, TILE_ROWS, batch):
            rows = range(start, start + batch)
            dens = density_rows(
                [dist[row : row + 1] for row in rows], mean_ref, coef_ref, base_ref
            )
            bias = dot_wide(weight_ref[...], dens) * LOG2E
            for row in rows:
                for tile in range(tiles):
                    at = ((row - start) * tiles + tile) * LANES
                    out_ref[first + tile, pl.ds(base + row, heads, stride=row_count), :] = (
                        bias[:, at : at + LANES]
                        + mask[row : row + 1, tile * LANES : (tile + 1) * LANES]
                    )

    def one_tile(tile_index, carry):
        base = pl.multiple_of(tile_index * TILE_ROWS, TILE_ROWS)
        flag = flag_ref[micro, pl.program_id(0) * (row_count // TILE_ROWS) + tile_index]

        @pl.when(flag != 1)
        def _():
            compute(base, 0, long_tiles, 2)

        @pl.when(flag == 1)
        def _():
            fill(base, 0, long_tiles)

        @pl.when(flag != 0)
        def _():
            compute(base, long_tiles, all_tiles - long_tiles, TILE_ROWS)

        @pl.when(flag == 0)
        def _():
            fill(base, long_tiles, all_tiles - long_tiles)

        return carry

    lax.fori_loop(0, row_count // TILE_ROWS, one_tile, 0)


def pair_bias(micro, earlier, flags, dist, mask, mean_wide, coef_wide, base_wide, weight):
    micro_count, row_count, columns = dist.shape
    heads, kernels = weight.shape
    blocks = row_count // ROW_BLOCK
    block = pl.BlockSpec((None, ROW_BLOCK, columns), lambda i: (micro, i, 0))
    wide = pl.BlockSpec((kernels, LANES), lambda i: (0, 0))
    shape = (micro_count, blocks, columns // LANES, heads * ROW_BLOCK, LANES)
    operands = [flags, dist, mask, mean_wide, coef_wide, base_wide, weight]
    specs = [
        pl.BlockSpec(memory_space=pltpu.SMEM),
        block,
        block,
        wide,
        wide,
        wide,
        pl.BlockSpec((heads, kernels), lambda i: (0, 0)),
    ]
    if earlier is not None:
        operands.append(earlier)
        specs.append(pl.BlockSpec(memory_space=pl.ANY))
    return pl.pallas_call(
        functools.partial(bias_kernel, micro),
        grid=(blocks,),
        in_specs=specs,
        out_specs=pl.BlockSpec((None, None) + shape[2:], lambda i: (micro, i, 0, 0, 0)),
        out_shape=jax.ShapeDtypeStruct(shape, f32),
        input_output_aliases={} if earlier is None else {7: 0},
        compiler_params=pltpu.CompilerParams(vmem_limit_bytes=VMEM_LIMIT),
        cost_estimate=cost(11),
        name="pair_bias",
    )(*operands)


def two_parts(value):
    high = value.astype(bf16)
    return high, (value - high.astype(f32)).astype(bf16)


def pair_grad_kernel(micro, flag_ref, dist_ref, score_ref, mean_ref, coef_ref, out_ref):
    row_count, columns = dist_ref.shape
    heads = score_ref.shape[1] // row_count
    long_tiles = PROTEIN_ROWS // LANES
    all_tiles = columns // LANES

    @pl.when(pl.program_id(0) == 0)
    def _():
        out_ref[...] = jnp.zeros_like(out_ref)

    def compute(base, first, tiles, batch):
        total = out_ref[...]
        span = slice(first * LANES, (first + tiles) * LANES)
        dist = dist_ref[pl.ds(base, TILE_ROWS), span]
        for start in range(0, TILE_ROWS, batch):
            rows = range(start, start + batch)
            dens = density_rows([dist[row : row + 1] for row in rows], mean_ref, coef_ref, None)
            score = jnp.concatenate(
                [
                    score_ref[first + tile, pl.ds(base + row, heads, stride=row_count), :]
                    for row in rows
                    for tile in range(tiles)
                ],
                axis=1,
            ).astype(bf16)
            far = jnp.concatenate([dist[row : row + 1] for row in rows], axis=1) - CENTRE
            once = score.astype(f32) * far
            stack = jnp.concatenate([score, *two_parts(once), *two_parts(once * far)], axis=0)
            total = total + dot_nt(stack, dens)
        out_ref[...] = total

    def one_tile(tile_index, carry):
        base = pl.multiple_of(tile_index * TILE_ROWS, TILE_ROWS)
        flag = flag_ref[micro, pl.program_id(0) * (row_count // TILE_ROWS) + tile_index]

        @pl.when(flag != 1)
        def _():
            compute(base, 0, long_tiles, 2)

        @pl.when(flag != 0)
        def _():
            compute(base, long_tiles, all_tiles - long_tiles, TILE_ROWS)

        return carry

    lax.fori_loop(0, row_count // TILE_ROWS, one_tile, 0)


def pair_grads(micro, flags, dist, score_cot, mean_wide, coef_wide):
    columns = dist.shape[2]
    blocks = score_cot.shape[1]
    kernels = mean_wide.shape[0]
    heads = score_cot.shape[3] // ROW_BLOCK
    wide = pl.BlockSpec((kernels, LANES), lambda i: (0, 0))
    return pl.pallas_call(
        functools.partial(pair_grad_kernel, micro),
        grid=(blocks,),
        in_specs=[
            pl.BlockSpec(memory_space=pltpu.SMEM),
            pl.BlockSpec((None, ROW_BLOCK, columns), lambda i: (micro, i, 0)),
            pl.BlockSpec((None, None) + score_cot.shape[2:], lambda i: (micro, i, 0, 0, 0)),
            wide,
            wide,
        ],
        out_specs=pl.BlockSpec((5 * heads, kernels), lambda i: (0, 0)),
        out_shape=jax.ShapeDtypeStruct((5 * heads, kernels), f32),
        compiler_params=pltpu.CompilerParams(vmem_limit_bytes=VMEM_LIMIT),
        cost_estimate=cost(14),
        name="pair_grads",
    )(flags, dist, score_cot, mean_wide, coef_wide)


def head_stack(tile):
    lane_head = lax.broadcasted_iota(jnp.int32, (1, LANES), 1) // HEAD_PAD
    return jnp.concatenate(
        [
            jnp.where(lane_head == head, tile, jnp.zeros_like(tile))
            for head in range(LANES // HEAD_PAD)
        ],
        axis=0,
    )


def head_merge(stacked, row_count):
    lane_head = lax.broadcasted_iota(jnp.int32, (1, LANES), 1) // HEAD_PAD
    merged = stacked[:row_count]
    for head in range(1, LANES // HEAD_PAD):
        merged = jnp.where(
            lane_head == head, stacked[head * row_count : (head + 1) * row_count], merged
        )
    return merged


def attend_kernel(scale, query_ref, key_ref, value_ref, bias_ref, prob_ref, out_ref):
    row_count = query_ref.shape[0]
    blocks, tiles = bias_ref.shape[:2]
    heads = LANES // HEAD_PAD
    stack = heads * row_count
    for group in range(query_ref.shape[1] // LANES):
        lanes = slice(group * LANES, (group + 1) * LANES)
        rows = slice(group * stack, (group + 1) * stack)
        scores = dot_nt(head_stack(query_ref[:, lanes]), key_ref[:, lanes]) * scale
        bias = [
            [
                bias_ref[block, tile, head * ROW_BLOCK : (head + 1) * ROW_BLOCK]
                for head in range(group * heads, (group + 1) * heads)
                for block in range(blocks)
            ]
            for tile in range(tiles)
        ]
        scores = scores + jnp.concatenate([jnp.concatenate(b, axis=0) for b in bias], axis=1)
        exps = jnp.exp2(scores - jnp.max(scores, axis=1, keepdims=True))
        probs = (exps * (1.0 / jnp.sum(exps, axis=1, keepdims=True))).astype(bf16)
        prob_ref[rows] = probs
        merged = head_merge(dot_wide(probs, value_ref[:, lanes]), row_count)
        out_ref[:, lanes] = merged.astype(bf16)


def attend(query, both, bias, scale):
    micro_count, row_count, width = query.shape
    columns = both.shape[1]
    wide = PER_STEP * LANES
    groups = width // wide
    heads = PER_STEP * (LANES // HEAD_PAD)
    stack = heads * row_count
    own = pl.BlockSpec((None, row_count, wide), lambda m, g: (m, 0, g))
    whole = pl.BlockSpec((None, columns, wide), lambda m, g: (m, 0, g))
    later = pl.BlockSpec((None, columns, wide), lambda m, g: (m, 0, groups + g))
    return pl.pallas_call(
        functools.partial(attend_kernel, scale),
        grid=(micro_count, groups),
        in_specs=[
            own,
            whole,
            later,
            pl.BlockSpec(
                (None, row_count // ROW_BLOCK, columns // LANES, heads * ROW_BLOCK, LANES),
                lambda m, g: (m, 0, 0, g, 0),
            ),
        ],
        out_specs=[pl.BlockSpec((None, stack, columns), lambda m, g: (m, g, 0)), own],
        out_shape=[
            jax.ShapeDtypeStruct((micro_count, groups * stack, columns), bf16),
            jax.ShapeDtypeStruct((micro_count, row_count, width), bf16),
        ],
        compiler_params=pltpu.CompilerParams(vmem_limit_bytes=VMEM_LIMIT),
        cost_estimate=cost(30),
        name="attend",
    )(query, both, both, bias)


def attend_back_kernel(
    scale,
    query_ref,
    key_ref,
    value_ref,
    cot_ref,
    prob_ref,
    score_ref,
    query_cot_ref,
    key_cot_ref,
    value_cot_ref,
):
    row_count = query_ref.shape[0]
    blocks, tiles = score_ref.shape[:2]
    heads = LANES // HEAD_PAD
    stack = heads * row_count
    for group in range(query_ref.shape[1] // LANES):
        lanes = slice(group * LANES, (group + 1) * LANES)
        rows = slice(group * stack, (group + 1) * stack)
        cot_stack = head_stack(cot_ref[:, lanes])
        low_probs = prob_ref[rows]
        probs = low_probs.astype(f32)
        weighted = probs * dot_nt(cot_stack, value_ref[:, lanes])
        score_cot = weighted - probs * jnp.sum(weighted, axis=1, keepdims=True)
        for head in range(heads):
            to = slice((group * heads + head) * ROW_BLOCK, (group * heads + head + 1) * ROW_BLOCK)
            for block in range(blocks):
                at = head * row_count + block * ROW_BLOCK
                for tile in range(tiles):
                    score_ref[block, tile, to] = score_cot[
                        at : at + ROW_BLOCK, tile * LANES : (tile + 1) * LANES
                    ]
        low = score_cot.astype(bf16)
        merged = head_merge(dot_wide(low, key_ref[:, lanes]), row_count)
        query_cot_ref[:, lanes] = (merged * scale).astype(bf16)
        key_cot = dot_tn(low, head_stack(query_ref[:, lanes])) * scale
        key_cot_ref[:, lanes] = key_cot.astype(bf16)
        value_cot_ref[:, lanes] = dot_tn(low_probs, cot_stack).astype(bf16)


def attend_back(query, both, cot, probs, scale):
    micro_count, row_count, width = query.shape
    columns = both.shape[1]
    block = (
        row_count // ROW_BLOCK,
        columns // LANES,
        PER_STEP * (LANES // HEAD_PAD) * ROW_BLOCK,
        LANES,
    )
    wide = PER_STEP * LANES
    groups = width // wide
    heads = PER_STEP * (LANES // HEAD_PAD)
    stack = heads * row_count
    own = pl.BlockSpec((None, row_count, wide), lambda m, g: (m, 0, g))
    whole = pl.BlockSpec((None, columns, wide), lambda m, g: (m, 0, g))
    later = pl.BlockSpec((None, columns, wide), lambda m, g: (m, 0, groups + g))
    return pl.pallas_call(
        functools.partial(attend_back_kernel, scale),
        grid=(micro_count, groups),
        in_specs=[
            own,
            whole,
            later,
            own,
            pl.BlockSpec((None, stack, columns), lambda m, g: (m, g, 0)),
        ],
        out_specs=[
            pl.BlockSpec((None,) + block, lambda m, g: (m, 0, 0, g, 0)),
            own,
            whole,
            whole,
        ],
        out_shape=[
            jax.ShapeDtypeStruct(
                (micro_count,) + block[:2] + (groups * block[2], LANES), f32
            ),
            jax.ShapeDtypeStruct((micro_count, row_count, width), bf16),
            jax.ShapeDtypeStruct((micro_count, columns, width), bf16),
            jax.ShapeDtypeStruct((micro_count, columns, width), bf16),
        ],
        compiler_params=pltpu.CompilerParams(vmem_limit_bytes=VMEM_LIMIT),
        cost_estimate=cost(35),
        name="attend_back",
    )(query, both, both, cot, probs)


def spans(start, stop, width):
    pieces = []
    at = start
    while at < stop:
        block = at // width
        last = min(stop, (block + 1) * width)
        pieces.append((block, at - block * width, last - block * width, at - start))
        at = last
    return pieces


def roll_matrix(size, shift):
    row = lax.broadcasted_iota(jnp.int32, (size, size), 0) + shift
    row = jnp.where(row >= size, row - size, row)
    column = lax.broadcasted_iota(jnp.int32, (size, size), 1)
    return jnp.where(row == column, 1.0, 0.0).astype(bf16)


def weight_loads(me, mine, other, weights, sems, first):
    core = me & 1
    return [
        pltpu.make_async_copy(
            src.at[i], weights.at[2 * i + (core ^ side)], sems.at[first + 2 * side + i]
        )
        for side, src in enumerate((mine, other))
        for i in range(2)
    ]


def project_kernel(
    at_ref,
    a0,
    a1,
    a2,
    a3,
    w0,
    w1,
    query_out,
    both_out,
    rolled_out,
    rows,
    weights,
    query_ref,
    both_ref,
    rolled_ref,
    sems,
    out_sems,
):
    micro_count, group_rows, width = rolled_ref.shape
    tok_rows = group_rows // 4
    wide = query_ref.shape[2]
    block_width = weights.shape[2]
    me = at_ref[0]
    row_copies = [
        pltpu.make_async_copy(src, rows.at[me ^ r], sems.at[r])
        for r, src in enumerate((a0, a1, a2, a3))
    ]
    weight_copies = weight_loads(me, w0, w1, weights, sems, 4)
    for copy in row_copies + weight_copies:
        copy.start()
    for copy in row_copies:
        copy.wait()
    for micro in range(micro_count):
        group = jnp.concatenate(
            [rows[s, micro * tok_rows : (micro + 1) * tok_rows, :] for s in range(4)], axis=0
        )
        turn = roll_matrix(group_rows, at_ref[1 + micro])
        rolled_ref[micro] = dot_wide(turn, group).astype(bf16)

    def leave(micro):
        return [
            pltpu.make_async_copy(ref.at[micro], out.at[micro], out_sems.at[3 * micro + i])
            for i, (ref, out) in enumerate(
                ((query_ref, query_out), (both_ref, both_out), (rolled_ref, rolled_out))
            )
        ]

    for copy in weight_copies:
        copy.wait()

    def one(micro, carry):
        own = rows[me, pl.ds(micro * tok_rows, tok_rows), :]
        for block, first, last, offset in spans(0, wide, block_width):
            query_ref[micro, :, offset : offset + last - first] = dot_wide(
                own, weights[block, :, first:last]
            ).astype(bf16)
        group = rolled_ref[micro]
        for block, first, last, offset in spans(wide, 3 * wide, block_width):
            both_ref[micro, :, offset : offset + last - first] = dot_wide(
                group, weights[block, :, first:last]
            ).astype(bf16)
        for copy in leave(micro):
            copy.start()
        return carry

    lax.fori_loop(0, micro_count, one, 0)
    for micro in range(micro_count):
        for copy in leave(micro):
            copy.wait()


def project(places, rows, weights, micro_count, wide):
    total_rows, width = rows[0].shape
    tok_rows = total_rows // micro_count
    group_rows = 4 * tok_rows
    block_width = weights[0].shape[2]
    return pl.pallas_call(
        project_kernel,
        in_specs=[pl.BlockSpec(memory_space=pltpu.SMEM)]
        + [pl.BlockSpec(memory_space=pl.ANY)] * 6,
        out_specs=[pl.BlockSpec(memory_space=pl.ANY)] * 3,
        out_shape=[
            jax.ShapeDtypeStruct((micro_count, tok_rows, wide), bf16),
            jax.ShapeDtypeStruct((micro_count, group_rows, 2 * wide), bf16),
            jax.ShapeDtypeStruct((micro_count, group_rows, width), bf16),
        ],
        scratch_shapes=[
            pltpu.VMEM((4, total_rows, width), bf16),
            pltpu.VMEM((4, width, block_width), bf16),
            pltpu.VMEM((micro_count, tok_rows, wide), bf16),
            pltpu.VMEM((micro_count, group_rows, 2 * wide), bf16),
            pltpu.VMEM((micro_count, group_rows, width), bf16),
            pltpu.SemaphoreType.DMA((8,)),
            pltpu.SemaphoreType.DMA((3 * micro_count,)),
        ],
        compiler_params=pltpu.CompilerParams(vmem_limit_bytes=VMEM_LIMIT),
        cost_estimate=cost(10),
        name="project",
    )(places, *rows, *weights)


def project_back_kernel(
    at_ref,
    query_ref,
    key_ref,
    value_ref,
    rolled_ref,
    own_ref,
    w0,
    w1,
    own_cot_ref,
    group_keep_ref,
    group_give_ref,
    grad_keep_ref,
    grad_give_ref,
    weights,
    stage,
    sems,
):
    micro_count, group_rows, width = rolled_ref.shape
    tok_rows = group_rows // 4
    wide = query_ref.shape[2]
    block_width = weights.shape[2]
    me = at_ref[0]
    weight_copies = weight_loads(me, w0, w1, weights, sems, 0)
    for copy in weight_copies:
        copy.start()
    grad_copies = []
    own_turned = own_ref[...].T
    rolled_turned = rolled_ref[...].reshape(-1, width).T
    for block in range(4):
        low, high = block * block_width, (block + 1) * block_width
        parts = []
        for which, cot_ref in enumerate((query_ref, key_ref, value_ref)):
            first = max(low, which * wide) - which * wide
            last = min(high, (which + 1) * wide) - which * wide
            if first < last:
                left = own_turned if which == 0 else rolled_turned
                right = cot_ref[...].reshape(-1, wide)[:, first:last]
                parts.append(dot_wide(left, right).astype(bf16))
        stage[block] = parts[0] if len(parts) == 1 else jnp.concatenate(parts, axis=1)
        for leaves, target in enumerate((grad_keep_ref, grad_give_ref)):
            copy = pltpu.make_async_copy(
                stage.at[block], target.at[(me ^ block) >> 1], sems.at[4 + block]
            )
            grad_copies.append((((me ^ block) & 1) == leaves, copy))

            @pl.when(((me ^ block) & 1) == leaves)
            def _():
                copy.start()

    for copy in weight_copies:
        copy.wait()

    def one(micro, carry):
        total = None
        for block, first, last, offset in spans(0, wide, block_width):
            part = dot_nt(
                query_ref[micro, :, offset : offset + last - first], weights[block, :, first:last]
            )
            total = part if total is None else total + part
        own_cot_ref[micro] = total
        total = None
        for block, first, last, offset in spans(wide, 3 * wide, block_width):
            source = key_ref if offset < wide else value_ref
            at = offset if offset < wide else offset - wide
            end = at + last - first
            pieces = [(source, at, end, first)]
            if offset < wide < offset + last - first:
                cut = wide - offset
                pieces = [(key_ref, offset, wide, first), (value_ref, 0, end - wide, first + cut)]
            for ref, begin, stop, column in pieces:
                part = dot_nt(
                    ref[micro, :, begin:stop], weights[block, :, column : column + stop - begin]
                )
                total = part if total is None else total + part
        turn = roll_matrix(group_rows, at_ref[1 + micro])
        back = dot_tn(turn, total.astype(bf16)).astype(bf16)
        for s in range(4):
            for leaves, target in enumerate((group_keep_ref, group_give_ref)):

                @pl.when(((me ^ s) & 1) == leaves)
                def _():
                    target[(me ^ s) >> 1, pl.ds(micro * tok_rows, tok_rows), :] = back[
                        s * tok_rows : (s + 1) * tok_rows
                    ]

        return carry

    lax.fori_loop(0, micro_count, one, 0)
    for started, copy in grad_copies:

        @pl.when(started)
        def _():
            copy.wait()


def project_back(places, query_cot, key_cot, value_cot, rolled, own, weights):
    micro_count, group_rows, width = rolled.shape
    tok_rows = group_rows // 4
    block_width = weights[0].shape[2]
    whole = pl.BlockSpec(memory_space=pltpu.VMEM)
    away = pl.BlockSpec(memory_space=pl.ANY)
    return pl.pallas_call(
        project_back_kernel,
        in_specs=[pl.BlockSpec(memory_space=pltpu.SMEM)] + [whole] * 5 + [away] * 2,
        out_specs=[whole, whole, whole, away, away],
        out_shape=[jax.ShapeDtypeStruct((micro_count, tok_rows, width), f32)]
        + [jax.ShapeDtypeStruct((2, micro_count * tok_rows, width), bf16)] * 2
        + [jax.ShapeDtypeStruct((2, width, block_width), bf16)] * 2,
        scratch_shapes=[
            pltpu.VMEM((4, width, block_width), bf16),
            pltpu.VMEM((4, width, block_width), bf16),
            pltpu.SemaphoreType.DMA((8,)),
        ],
        compiler_params=pltpu.CompilerParams(vmem_limit_bytes=VMEM_LIMIT),
        cost_estimate=cost(14),
        name="project_back",
    )(places, query_cot, key_cot, value_cot, rolled, own, *weights)


CHUNKS = 8


def dense_kernel(
    att_ref,
    start_ref,
    cot_ref,
    gain_ref,
    place_ref,
    big_ref,
    out_ref,
    mid_cot_ref,
    att_cot_ref,
    gain_cot_ref,
    grad_ref,
    up_v,
    down_v,
    output_v,
    mid_v,
    normed_v,
    inv_v,
    ffn_v,
    branch_v,
    total_v,
    back_v,
    up_s,
    cot_s,
    gelu_v,
    cot_v,
    up_stage,
    down_stage,
    output_stage,
    zero_v,
    sems,
    grad_sems,
):
    rows, width = start_ref.shape
    own = width // CHUNKS
    third = own // 3
    pair = CHUNKS // 4
    step = rows // 3
    output_copy = pltpu.make_async_copy(
        big_ref.at[:, pl.ds(0, 3), pl.ds(2 * own, third)], output_v, sems.at[8]
    )

    def up_copy(j):
        return pltpu.make_async_copy(big_ref.at[:, j, pl.ds(0, own)], up_v.at[j], sems.at[j])

    def down_copy(j):
        return pltpu.make_async_copy(
            big_ref.at[pl.ds(j * pair, pair), :, pl.ds(own, own)], down_v.at[j], sems.at[4 + j]
        )

    def up_out(j):
        return pltpu.make_async_copy(
            up_stage.at[j], grad_ref.at[:, j, pl.ds(0, own)], grad_sems.at[j]
        )

    def down_out(j):
        return pltpu.make_async_copy(
            down_stage.at[j],
            grad_ref.at[pl.ds(j * pair, pair), :, pl.ds(own, own)],
            grad_sems.at[4 + j],
        )

    output_copy.start()
    for j in range(4):
        up_copy(j).start()
        down_copy(j).start()
    zero_v[...] = jnp.zeros_like(zero_v)
    zero_copy = pltpu.make_async_copy(
        zero_v, grad_ref.at[:, 3, pl.ds(2 * own, third)], grad_sems.at[8]
    )
    zero_copy.start()
    att = dot_nt(att_ref[...], place_ref[...]).astype(bf16)
    branch_v[...] = cot_ref[...].astype(bf16)
    output_copy.wait()
    output_w = output_v[...].reshape(width, width)
    gain = gain_ref[...]
    mid_v[...] = start_ref[...] + dot_wide(att, output_w)
    for part in range(3):
        at = slice(part * step, (part + 1) * step)
        mid = mid_v[at]
        centre = mid - jnp.mean(mid, axis=1, keepdims=True)
        inv_std = lax.rsqrt(jnp.mean(centre * centre, axis=1, keepdims=True) + NORM_EPS)
        normed = centre * inv_std
        normed_v[at] = normed
        inv_v[at] = jnp.broadcast_to(inv_std, (step, LANES))
        ffn_v[at] = (normed * gain).astype(bf16)
    ffn_turned = ffn_v[...].T
    total_v[...] = mid_v[...]
    back_v[...] = jnp.zeros_like(back_v)

    def one(j, carry):
        up_copy(j).wait()
        down_copy(j).wait()
        up_w = up_v[j].reshape(width, width)
        down_w = down_v[j].reshape(width, width)
        up_s[...] = dot_wide(ffn_v[...], up_w)
        cot_s[...] = dot_nt(branch_v[...], down_w)
        gelus, cots = [], []
        for start in range(0, rows, 64):
            at = slice(start, start + 64)
            up = up_s[at]
            square = up * up
            root = math.sqrt(2.0 / math.pi)
            bend = jnp.tanh(up * (root + (root * 0.044715) * square))
            half = 0.5 + 0.5 * bend
            slope = half + up * (0.5 - 0.5 * bend * bend) * (
                root + (root * 3 * 0.044715) * square
            )
            gelus.append((up * half).astype(bf16))
            cots.append((cot_s[at] * slope).astype(bf16))
        gelu = jnp.concatenate(gelus, axis=0)
        cot = jnp.concatenate(cots, axis=0)
        gelu_v[...] = gelu
        cot_v[...] = cot
        total_v[...] += dot_wide(gelu_v[...], down_w)
        back_v[...] += dot_nt(cot_v[...], up_w)
        up_stage[j] = dot_wide(ffn_turned, cot_v[...]).astype(bf16).reshape(up_stage.shape[1:])
        up_out(j).start()
        down_stage[j] = (
            dot_tn(gelu_v[...], branch_v[...]).astype(bf16).reshape(down_stage.shape[1:])
        )
        down_out(j).start()
        return carry

    lax.fori_loop(0, 4, one, 0)
    out_ref[...] = total_v[...].astype(bf16)
    gain_cot = jnp.zeros((1, width), f32)
    for part in range(3):
        at = slice(part * step, (part + 1) * step)
        back = back_v[at]
        normed = normed_v[at]
        gain_cot = gain_cot + jnp.sum(back * normed, axis=0, keepdims=True)
        scaled = back * gain
        mid_cot = cot_ref[at] + inv_v[at][:, :1] * (
            scaled
            - jnp.mean(scaled, axis=1, keepdims=True)
            - normed * jnp.mean(scaled * normed, axis=1, keepdims=True)
        )
        mid_cot_ref[at] = mid_cot
        cot_v[at] = mid_cot.astype(bf16)
    gain_cot_ref[...] = gain_cot
    att_cot = dot_nt(cot_v[...], output_w).astype(bf16)
    att_cot_ref[...] = dot_wide(att_cot, place_ref[...]).astype(bf16)
    output_stage[...] = dot_tn(att, cot_v[...]).astype(bf16).reshape(output_stage.shape)
    output_out = pltpu.make_async_copy(
        output_stage, grad_ref.at[:, pl.ds(0, 3), pl.ds(2 * own, third)], grad_sems.at[9]
    )
    output_out.start()
    for j in range(4):
        up_out(j).wait()
        down_out(j).wait()
    output_out.wait()
    zero_copy.wait()


def dense(attended, start, out_cot, gain, place_heads, big):
    rows, width = start.shape
    wide = attended.shape[1]
    own = width // CHUNKS
    third = own // 3
    pair = CHUNKS // 4
    whole = pl.BlockSpec(memory_space=pltpu.VMEM)
    away = pl.BlockSpec(memory_space=pl.ANY)
    return pl.pallas_call(
        dense_kernel,
        in_specs=[whole] * 5 + [away],
        out_specs=[whole] * 4 + [away],
        out_shape=[
            jax.ShapeDtypeStruct((rows, width), bf16),
            jax.ShapeDtypeStruct((rows, width), f32),
            jax.ShapeDtypeStruct((rows, wide), bf16),
            jax.ShapeDtypeStruct((1, width), f32),
            jax.ShapeDtypeStruct(big.shape, bf16),
        ],
        scratch_shapes=[
            pltpu.VMEM((4, CHUNKS, own, width), bf16),
            pltpu.VMEM((4, pair, 4, own, width), bf16),
            pltpu.VMEM((CHUNKS, 3, third, width), bf16),
            pltpu.VMEM((rows, width), f32),
            pltpu.VMEM((rows, width), f32),
            pltpu.VMEM((rows, LANES), f32),
            pltpu.VMEM((rows, width), bf16),
            pltpu.VMEM((rows, width), bf16),
            pltpu.VMEM((rows, width), f32),
            pltpu.VMEM((rows, width), f32),
            pltpu.VMEM((rows, width), f32),
            pltpu.VMEM((rows, width), f32),
            pltpu.VMEM((rows, width), bf16),
            pltpu.VMEM((rows, width), bf16),
            pltpu.VMEM((4, CHUNKS, own, width), bf16),
            pltpu.VMEM((4, pair, 4, own, width), bf16),
            pltpu.VMEM((CHUNKS, 3, third, width), bf16),
            pltpu.VMEM((CHUNKS, third, width), bf16),
            pltpu.SemaphoreType.DMA((9,)),
            pltpu.SemaphoreType.DMA((10,)),
        ],
        compiler_params=pltpu.CompilerParams(vmem_limit_bytes=VMEM_LIMIT),
        cost_estimate=cost(25),
        name="dense",
    )(attended, start, out_cot, gain, place_heads, big)


def place_matrix(source, piece, padded):
    index = jnp.arange(source, dtype=jnp.int32)
    target = (index // piece) * padded + index % piece
    spots = jnp.arange(source // piece * padded, dtype=jnp.int32)
    return (target[:, None] == spots[None, :]).astype(bf16)


def dot_low(left, right):
    return jnp.dot(left, right, preferred_element_type=f32).astype(bf16)


def roll_rows(value, shift, axis):
    size = value.shape[axis]
    twice = jnp.concatenate([value, value], axis=axis)
    return lax.dynamic_slice_in_dim(twice, shift, size, axis)


def gather_shards(shard):
    return lax.all_gather(shard, "fsdp", axis=0, tiled=True)


def reduce_shards(grad):
    part = lax.psum_scatter(grad, "fsdp", scatter_dimension=0, tiled=True)
    return lax.psum(part.astype(bf16), "seq").astype(f32)[0]


LINE = 4


def place():
    fsdp_index, seq_index = lax.axis_index("fsdp"), lax.axis_index("seq")
    return fsdp_index // 2, fsdp_index % 2, seq_index // 2, seq_index % 2


def flip(value, axis, bit):
    return lax.ppermute(value, axis, [(i, i ^ bit) for i in range(lax.axis_size(axis))])


def along_line(value, step):
    pairs = [
        (z * 2 + y, (z + step) % LINE * 2 + y) for z in range(LINE) for y in range(2)
    ]
    return lax.ppermute(value, "fsdp", pairs)


def line_gather(block, axis=0):
    z = place()[0]
    parts = [block] + [along_line(block, step) for step in range(1, LINE)]
    ring = jnp.stack([parts[-step % LINE] for step in range(LINE)] * 2, axis=axis)
    return lax.dynamic_slice_in_dim(ring, (LINE - z) % LINE, LINE, axis)


def in_line(parts, axis=0):
    z = place()[0]
    return jnp.stack(
        [lax.select_n((z + LINE - at) % LINE, *parts) for at in range(LINE)], axis=axis
    )


def pair_gather(value, bit_axis, bit, own_bit, axis=0):
    other = flip(value, bit_axis, bit)
    return jnp.stack(
        [jnp.where(own_bit == 0, value, other), jnp.where(own_bit == 0, other, value)], axis=axis
    )


def pair_reduce(value, bit_axis, bit, own_bit, axis=0):
    keep, give = pair_split(value, own_bit, axis)
    return add_low(keep, flip(give, bit_axis, bit))


def pair_split(value, own_bit, axis):
    keep = lax.dynamic_index_in_dim(value, own_bit, axis, keepdims=False)
    return keep, lax.dynamic_index_in_dim(value, 1 - own_bit, axis, keepdims=False)


def add_low(left, right):
    return (left.astype(f32) + right.astype(f32)).astype(left.dtype)


def line_reduce(value, *others):
    z = place()[0]
    total = lax.dynamic_index_in_dim(value, z, 0, keepdims=False).astype(f32)
    for step in range(1, LINE):
        give = lax.dynamic_index_in_dim(value, (z + step) % LINE, 0, keepdims=False)
        total = total + after(along_line(give, step), *others).astype(f32)
    return total


def fast_mesh():
    return (lax.axis_size("fsdp"), lax.axis_size("seq")) == (2 * LINE, 4)


def exact_parts(value):
    parts = []
    for _ in range(2):
        part = lax.reduce_precision(value, 8, 7)
        parts.append(part.astype(bf16))
        value = value - part
    return parts + [value.astype(bf16)]


def gather_small(small, stamps):
    if not fast_mesh():
        whole = lax.all_gather(small, "fsdp", axis=0)
        return whole, lax.all_gather(stamps, "fsdp", axis=0), whole
    parts = jnp.concatenate(exact_parts(stamps))
    row = jnp.pad(parts, (0, LANES - parts.shape[0]))[None]
    packed = jnp.concatenate([small, jnp.pad(row, ((0, 15), (0, 0)))], axis=0)
    line = line_gather(packed)
    packed = pair_gather(line, "fsdp", 1, place()[1], 1)
    packed = packed.reshape((2 * LINE,) + packed.shape[2:])
    count = stamps.shape[0]
    row = packed[:, small.shape[0]].astype(f32)
    stamps_all = row[:, :count] + row[:, count : 2 * count] + row[:, 2 * count : 3 * count]
    return packed[:, : small.shape[0]], stamps_all, line


def after(value, *others):
    if not others:
        return value
    return lax.optimization_barrier((value,) + others)[0]


def scatter_groups(value):
    if not fast_mesh():
        return lax.psum_scatter(value, "fsdp", scatter_dimension=0, tiled=True)[0], value
    y, core = place()[1], place()[3]
    half = value.shape[2] // 2
    value = lax.dynamic_slice_in_dim(value, core * half, half, 2)
    value = value.reshape((LINE, 2) + value.shape[1:])
    first = pair_reduce(value, "fsdp", 1, y, 1)
    value = line_reduce(first)
    other = flip(value, "seq", 1)
    value = jnp.concatenate(
        [jnp.where(core == 0, value, other), jnp.where(core == 0, other, value)], axis=1
    )
    return value, first


def gather_big(output_weight, up_weight, down_weight, *others):
    if not fast_mesh():
        up, down, output = (gather_shards(w) for w in (up_weight, down_weight, output_weight))
        width = output.shape[0]
        own = width // CHUNKS
        return join_big(
            up.reshape(CHUNKS, own, 4, width).transpose(0, 2, 1, 3),
            down.reshape(CHUNKS, 4, own, width),
            output.reshape(CHUNKS, own, width),
        )
    seq_index = lax.axis_index("seq")
    own, width = output_weight.shape
    third = own // 3
    quarter = jnp.concatenate(
        [
            lax.dynamic_slice_in_dim(up_weight, seq_index * width, width, 1),
            lax.dynamic_slice_in_dim(down_weight, seq_index * own, own, 0),
            lax.dynamic_slice_in_dim(
                jnp.pad(output_weight, ((0, third), (0, 0))), seq_index * third, third, 0
            ),
        ],
        axis=0,
    )
    big = lax.all_gather(after(quarter, *others), ("fsdp", "seq"), axis=0)
    return big.reshape((CHUNKS, 4) + quarter.shape)


def join_big(up, down, output):
    chunks, own, width = output.shape
    third = own // 3
    output = jnp.pad(output, ((0, 0), (0, third), (0, 0))).reshape(chunks, 4, third, width)
    return jnp.concatenate([up, down, output], axis=2)


def reduce_big(grad):
    chunks, quarters, rows, width = grad.shape
    own = width // CHUNKS
    if not fast_mesh():
        fsdp_count = lax.axis_size("fsdp")
        up = grad[:, :, :own].transpose(0, 2, 1, 3).reshape(fsdp_count, -1, 4 * width)
        down = grad[:, :, own : 2 * own].reshape(fsdp_count, -1, width)
        output = grad[:, :3, 2 * own :].reshape(fsdp_count, -1, width)
        return tuple(reduce_shards(g) for g in (up, down, output))
    total = lax.psum_scatter(
        grad.reshape(chunks * quarters, rows, width),
        ("fsdp", "seq"),
        scatter_dimension=0,
        tiled=True,
    )
    return total[0]


def four_ways(value):
    return value, flip(value, "seq", 1), flip(value, "seq", 2)


def fourth(three, *others):
    if not fast_mesh():
        return three
    value, near, across = three
    across = after(across, *others)
    return value, near, across, flip(across, "seq", 1)


def gather_projections(weight):
    columns = weight.shape[1] // 4
    if not fast_mesh():
        full = gather_shards(weight)
        blocks = [full[:, i * columns : (i + 1) * columns] for i in range(4)]
        return (jnp.stack(blocks[::2]), jnp.stack(blocks[1::2])), weight
    y, core = place()[1], place()[3]
    pair = jnp.stack(
        [
            lax.dynamic_slice_in_dim(weight, (core + 2 * i) * columns, columns, 1)
            for i in range(2)
        ]
    )
    line = line_gather(pair, 1)
    return (line, flip(line, "fsdp", 1)), line


def finish_projections(pair, *others):
    if not fast_mesh():
        return pair
    y = place()[1]
    line, other = pair
    other = after(other, *others)
    pair = jnp.stack(
        [jnp.where(y == 0, line, other), jnp.where(y == 0, other, line)], axis=2
    ).reshape(2, -1, line.shape[-1])
    return pair, flip(pair, "seq", 1)


def gather_group(value):
    if not fast_mesh():
        rows = lax.all_gather(value, "seq", axis=0)
        return tuple(rows[i] for i in range(4))
    return four_ways(value)


def in_order(keep, give):
    return keep[0], give[0], keep[1], give[1]


def reduce_group(keep, give):
    order = jnp.stack(in_order(keep, give))
    return lax.psum_scatter(order, "seq", scatter_dimension=0, tiled=True)[0].astype(f32)


def reduce_projections(keep, give):
    order = jnp.concatenate(in_order(keep, give), axis=1)
    return reduce_shards(order.reshape(lax.axis_size("fsdp"), -1, order.shape[1]))


def gather_finals(value, *others):
    x, core = place()[2:]
    width = value.shape[1]
    own = width // CHUNKS
    other = after(flip(value, "seq", 2), *others)
    total = jnp.stack([jnp.where(x == 0, value, other), jnp.where(x == 0, other, value)])
    total = pair_gather(total, "seq", 1, core, 1).astype(f32)
    total = total.reshape((4,) + value.shape)
    return (
        total[:, :own].transpose(1, 0, 2).reshape(own, -1),
        total[:, own : 2 * own].transpose(1, 0, 2).reshape(own, -1),
        total[:, 2 * own : 3 * own].reshape(-1, width),
        total[:3, 3 * own :].reshape(own, width),
    )


def join_lanes(value, lanes):
    return jnp.concatenate(
        [value[:, at : at + lanes] for at in range(0, value.shape[1], lanes)], axis=0
    )


def line_exchange(give, times, *others):
    z = place()[0]
    rows = give.shape[1]
    total = lax.dynamic_index_in_dim(give, z, 0, keepdims=False).astype(f32)
    parts = [times]
    for step in range(1, LINE):
        piece = lax.dynamic_index_in_dim(give, (z + step) % LINE, 0, keepdims=False)
        other = after(along_line(jnp.concatenate([piece, times], axis=0), step), *others)
        total = total + other[:rows].astype(f32)
        parts.append(other[rows:])
    return total, in_line(parts)


def pair_exchange(grad, times):
    y = place()[1]
    rows, lanes = grad.shape[2:]
    keep = lax.dynamic_index_in_dim(grad, y, 1, keepdims=False)
    give = lax.dynamic_index_in_dim(grad, 1 - y, 1, keepdims=False)
    give = jnp.concatenate([give.reshape(LINE * rows, lanes), times], axis=0)
    other = flip(give, "fsdp", 1)
    keep = add_low(keep, other[: LINE * rows].reshape(keep.shape))
    late = other[LINE * rows :]
    times = jnp.concatenate(
        [jnp.where(y == 0, times, late), jnp.where(y == 0, late, times)], axis=0
    )
    return keep, times


def body(
    hidden_in,
    row_types,
    lengths,
    noise_time,
    coords,
    residue_table,
    atom_table,
    time_weight,
    first_gain,
    query_weight,
    key_weight,
    value_weight,
    output_weight,
    kernel_mean,
    kernel_width,
    pair_weight,
    second_gain,
    up_weight,
    down_weight,
    force_weight,
    layer_cot,
    force_cot,
):
    seq_count = lax.axis_size("seq")
    fsdp_count = lax.axis_size("fsdp")
    seq_index = lax.axis_index("seq")
    micro_count, tok_rows, model_width = hidden_in.shape
    group_rows = tok_rows * seq_count
    own_kernels, head_count = pair_weight.shape
    kernels = own_kernels * fsdp_count
    head_dim = model_width // head_count
    inv_root = head_dim ** (-0.5)
    wide_heads = head_count * HEAD_PAD
    total_rows = micro_count * tok_rows
    residues, own_width = residue_table.shape
    types = residues + atom_table.shape[0]
    offset = seq_index * tok_rows

    small_rows = types + 16
    small = jnp.concatenate(
        [
            residue_table,
            atom_table,
            force_weight,
            first_gain[None],
            second_gain[None],
            jnp.zeros((small_rows - types - 5, own_width), bf16),
        ],
        axis=0,
    )
    small = jnp.pad(small, ((0, 0), (0, LANES - own_width)))
    kernel_rows = jnp.concatenate([pair_weight, kernel_mean[:, None], kernel_width[:, None]], axis=1)
    kernel_rows = jnp.pad(kernel_rows, ((0, 0), (0, LANES - head_count - 2)))
    big = gather_big(output_weight, up_weight, down_weight)
    small_all, stamps_all, small_line = gather_small(
        jnp.concatenate([small, kernel_rows], axis=0), noise_time[:, 0].reshape(-1)
    )
    head_place = place_matrix(model_width, head_dim, HEAD_PAD)
    qkv_weight = jnp.concatenate(
        [dot_low(w, head_place) for w in (query_weight, key_weight, value_weight)], axis=1
    )
    qkv_blocks, qkv_line = gather_projections(qkv_weight)
    kernel_all = small_all[:, small_rows:].reshape(kernels, LANES)
    pair_full = kernel_all[:, :head_count].astype(f32)
    mean_full = kernel_all[:, head_count].astype(f32)
    width_full = kernel_all[:, head_count + 1].astype(f32)
    spread = place_matrix(model_width, own_width, LANES)
    tables = dot_low(
        small_all[:, :small_rows].transpose(1, 0, 2).reshape(small_rows, fsdp_count * LANES),
        spread.T,
    )
    type_table = tables[:types]
    force_wide = tables[types : types + 3].astype(f32)
    gain_one = tables[types + 3].astype(f32)
    gain_two = tables[types + 4].astype(f32)

    coords = after(coords, small_line)
    doc_lengths = lengths[:, 0]
    documents = jnp.arange(doc_lengths.shape[1], dtype=jnp.int32)
    earlier = documents[:, None] <= documents[None, :]
    bounds = jnp.sum(jnp.where(earlier[None], doc_lengths[:, :, None], 0), axis=1)
    first_len = doc_lengths[:, 0]
    all_rows = jnp.arange(group_rows, dtype=jnp.int32)
    key_doc = jnp.sum((all_rows[None, :, None] >= bounds[:, None, :]).astype(jnp.int32), axis=2)
    query_doc = lax.dynamic_slice_in_dim(key_doc, offset, tok_rows, 1)
    query_pos = lax.dynamic_slice_in_dim(coords, offset, tok_rows, 2)
    roll_index = (all_rows[None, :] + first_len[:, None]) % group_rows
    rolled_doc = jnp.sum(
        (roll_index[:, :, None] >= bounds[:, None, :]).astype(jnp.int32), axis=2
    )
    rolled_pos = jnp.stack([roll_rows(coords[m], first_len[m], 1) for m in range(micro_count)])
    same_doc = query_doc[:, :, None] == rolled_doc[:, None, :]
    mask = jnp.where(same_doc, 0.0, -1e30).astype(f32)
    delta = query_pos[:, :, :, None] - rolled_pos[:, :, None, :]
    dist = jnp.sqrt(jnp.sum(delta * delta, axis=1))
    long_row = (query_doc == 1).reshape(micro_count, tok_rows // TILE_ROWS, TILE_ROWS)
    flags = jnp.where(
        jnp.all(long_row, axis=2), 0, jnp.where(jnp.any(long_row, axis=2), 2, 1)
    ).astype(jnp.int32)

    scale_k = 1.0 / (math.sqrt(2.0 * math.pi) * width_full)
    coef = (-0.5 * LOG2E) / (width_full * width_full)
    mean_wide = jnp.broadcast_to(mean_full[:, None], (kernels, LANES))
    coef_wide = jnp.broadcast_to(coef[:, None], (kernels, LANES))
    base_wide = jnp.broadcast_to(jnp.log2(scale_k)[:, None], (kernels, LANES))
    bias_weight = pair_full.T.astype(bf16)
    bias_args = (mask, mean_wide, coef_wide, base_wide, bias_weight)

    doc_hot = (
        query_doc[:, :, None] == jnp.arange(doc_lengths.shape[1], dtype=jnp.int32)
    ).astype(f32)
    type_hot = (
        row_types.reshape(total_rows)[:, None] == jnp.arange(types, dtype=jnp.int32)
    ).astype(bf16)
    time_low = sinus_columns(
        stamps_all, model_width, lax.axis_index("fsdp") * own_width, own_width
    )
    time_proj = dot_wide(time_low.reshape(-1, own_width), time_weight)
    time_proj, time_step = scatter_groups(time_proj.reshape(fsdp_count, -1, model_width))
    bias = pair_bias(0, None, flags, dist, *bias_args)
    bias = pair_bias(1, bias, flags, after(dist, qkv_line, time_step), *bias_args)
    time_proj = time_proj.reshape(micro_count, -1, model_width)
    start_state = (
        hidden_in.astype(f32)
        + dot_wide(type_hot, type_table).reshape(hidden_in.shape)
        + jnp.einsum("min,mnd->mid", doc_hot, time_proj, precision=EXACT)
    ).reshape(total_rows, model_width)
    normed_in, normed_one, inv_one = norm_forward(start_state, gain_one)
    attn_in = normed_in.astype(bf16)

    four = seq_index if fast_mesh() else 0
    places = jnp.concatenate([jnp.full((1,), four, jnp.int32), first_len])
    attn_rows = gather_group(attn_in)
    for micro in range(2, micro_count):
        bias = pair_bias(micro, bias, flags, after(dist, attn_in), *bias_args)
    attn_rows = fourth(attn_rows, bias)
    qkv_blocks = finish_projections(qkv_blocks, bias)
    queries, both, rolled = project(places, attn_rows, qkv_blocks, micro_count, wide_heads)
    probs, attended = attend(queries, both, bias, inv_root * LOG2E)
    forces_cot = force_cot.transpose(1, 0, 2).reshape(3, total_rows)
    out_grad = layer_cot.reshape(total_rows, model_width).astype(f32)
    for axis in range(3):
        out_grad = out_grad + forces_cot[axis][:, None] * force_wide[axis][None, :]
    layer_out, mid_grad, attended_grad, gain_two_grad, big_grad = dense(
        attended.reshape(total_rows, wide_heads),
        start_state,
        out_grad,
        gain_two[None],
        head_place,
        big,
    )
    big_sum = reduce_big(big_grad)
    forces = dot_nt(force_wide.astype(bf16), layer_out)
    forces = forces.reshape(3, micro_count, tok_rows).transpose(1, 0, 2)
    force_w_grad = jnp.dot(forces_cot, layer_out.astype(f32), precision=EXACT)

    score_cot, query_low, key_part, value_part = attend_back(
        queries,
        both,
        attended_grad.reshape(micro_count, tok_rows, wide_heads),
        probs,
        inv_root,
    )
    own_part, group_keep, group_give, qkv_keep, qkv_give = project_back(
        places, query_low, key_part, value_part, rolled, attn_in, qkv_blocks
    )

    def pair_sums(micro, earlier, *others):
        part = pair_grads(
            micro, flags, after(dist, earlier, *others), score_cot, mean_wide, coef_wide
        )
        return part if micro == 0 else earlier + part

    sums = pair_sums(0, group_give)
    if fast_mesh():
        group_other, qkv_other = (flip(v, "seq", 1) for v in (group_give, qkv_give))
        group_near = add_low(group_keep, after(group_other, sums))
        qkv_near = add_low(qkv_keep, after(qkv_other, sums))
        qkv_near = qkv_near.reshape((2, LINE, 2, -1) + qkv_near.shape[2:])
        pair_keep, pair_give = pair_split(qkv_near, place()[1], 2)
        group_other = flip(group_near[1], "seq", 2)
        qkv_other = flip(pair_give, "fsdp", 1)
        sums = pair_sums(1, sums, group_near, pair_give)
        group_sum = group_near[0].astype(f32) + after(group_other, sums).astype(f32)
    else:
        group_sum = reduce_group(group_keep, group_give)
    attn_in_grad = own_part.reshape(total_rows, model_width) + group_sum
    norm_part_one, gain_one_grad = norm_backward(attn_in_grad, normed_one, inv_one, gain_one)
    input_grad = mid_grad + norm_part_one

    input_low = input_grad.astype(bf16)
    type_grad = dot_tn(type_hot, input_low)
    time_cot = jnp.einsum(
        "min,mid->mnd",
        doc_hot.astype(bf16),
        input_low.reshape(micro_count, tok_rows, model_width),
        preferred_element_type=f32,
    ).reshape(-1, model_width)
    small_grad = jnp.concatenate(
        [
            type_grad,
            force_w_grad,
            gain_one_grad[None],
            gain_two_grad,
            jnp.zeros((small_rows - types - 5, model_width), f32),
        ],
        axis=0,
    )
    small_grad = dot_low(small_grad.astype(bf16), spread)
    small_grad = small_grad.reshape(small_rows, fsdp_count, LANES).transpose(1, 0, 2)

    def kernel_grads(sums):
        plain, once, once_low, twice, twice_low = (
            sums[k * head_count : (k + 1) * head_count].T for k in range(5)
        )
        centre = (mean_full - CENTRE)[:, None]
        once = once + once_low
        twice = twice + twice_low - centre * (2.0 * once - centre * plain)
        once = once - centre * plain
        pair_w_grad = plain * scale_k[:, None]
        inv_width = 1.0 / width_full
        mean_grad = jnp.sum(pair_full * once, axis=1) * scale_k * inv_width * inv_width
        width_grad = (
            jnp.sum(pair_full * (twice * (inv_width * inv_width)[:, None] - plain), axis=1)
            * scale_k
            * inv_width
        )
        grad = jnp.concatenate(
            [pair_w_grad, mean_grad[:, None], width_grad[:, None]], axis=1
        ).astype(bf16)
        grad = jnp.pad(grad, ((0, 0), (0, LANES - head_count - 2)))
        return grad.reshape(fsdp_count, own_kernels, LANES)

    if fast_mesh():
        small_other, time_other = (flip(v, "seq", 1) for v in (small_grad, time_cot))
        qkv_pair = add_low(pair_keep, after(qkv_other, small_grad, time_cot))
        qkv_other = flip(qkv_pair[1], "seq", 2)
        small_one, time_one = small_grad + small_other, time_cot + time_other
        for micro in range(2, micro_count):
            sums = pair_sums(micro, sums, qkv_pair, small_one, time_one)
        small_other, time_other = (flip(v, "seq", 2) for v in (small_one, time_one))
        qkv_far = add_low(qkv_pair[0], after(qkv_other, sums))
        kernel_grad = kernel_grads(after(sums, qkv_far))
        for bit in (1, 2):
            kernel_grad = kernel_grad + flip(kernel_grad, "seq", bit)
        small_two = small_one + after(small_other, sums)
        time_two = time_one + after(time_other, sums)
        small_two = jnp.concatenate([small_two, kernel_grad], axis=1)
        small_two = small_two.reshape((LINE, 2) + small_two.shape[1:])
        time_two = join_lanes(time_two.astype(bf16), LANES)
        small_half, time_pair = pair_exchange(small_two, time_two)
        qkv_own = line_reduce(qkv_far, small_half, time_pair).astype(bf16)
        finals = jnp.concatenate([qkv_own, big_sum], axis=0)
        small_sum, time_cots = line_exchange(small_half, time_pair, finals)
        time_cots = time_cots.reshape(
            fsdp_count, model_width // LANES, -1, LANES
        ).transpose(0, 2, 1, 3)
    else:
        for micro in range(1, micro_count):
            sums = pair_sums(micro, sums)
        small_sum = reduce_shards(jnp.concatenate([small_grad, kernel_grads(sums)], axis=1))
        time_cots = lax.all_gather(lax.psum(time_cot, "seq").astype(bf16), "fsdp", axis=0)
        finals = (reduce_projections(qkv_keep, qkv_give),) + big_sum
    row_sum = small_sum[:small_rows, :own_width]
    kernel_sum = small_sum[small_rows:]
    time_sum = dot_tn(time_low.reshape(-1, own_width), time_cots.reshape(-1, model_width))
    if fast_mesh():
        finals = gather_finals(finals, small_sum, time_cots)
    qkv_sum, up_sum, down_sum, output_sum = finals
    qkv_low = join_lanes(qkv_sum.astype(bf16), wide_heads)
    query_sum, key_sum, value_sum = dot_nt(qkv_low, head_place).reshape(3, -1, model_width)
    return (
        layer_out.reshape(hidden_in.shape),
        forces,
        input_grad.reshape(hidden_in.shape),
        row_sum[:residues],
        row_sum[residues:types],
        time_sum,
        row_sum[types + 3],
        query_sum,
        key_sum,
        value_sum,
        output_sum,
        kernel_sum[:, head_count],
        kernel_sum[:, head_count + 1],
        kernel_sum[:, :head_count],
        row_sum[types + 4],
        up_sum,
        down_sum,
        row_sum[types : types + 3],
    )


def solution(mesh):
    rows = ("fsdp", "seq")
    return jax.shard_map(
        body,
        mesh=mesh,
        in_specs=(
            P(None, rows, None),
            P(None, rows),
            P(None, "fsdp", None),
            P(None, "fsdp", None),
            P(None, None, "fsdp"),
            P(None, "fsdp"),
            P(None, "fsdp"),
            P("fsdp", None),
            P("fsdp"),
            P("fsdp", None),
            P("fsdp", None),
            P("fsdp", None),
            P("fsdp", None),
            P("fsdp"),
            P("fsdp"),
            P("fsdp", None),
            P("fsdp"),
            P("fsdp", None),
            P("fsdp", None),
            P(None, "fsdp"),
            P(None, rows, None),
            P(None, None, rows),
        ),
        out_specs=(
            P(None, rows, None),
            P(None, None, rows),
            P(None, rows, None),
            P(None, "fsdp"),
            P(None, "fsdp"),
            P("fsdp", None),
            P("fsdp"),
            P("fsdp", None),
            P("fsdp", None),
            P("fsdp", None),
            P("fsdp", None),
            P("fsdp"),
            P("fsdp"),
            P("fsdp", None),
            P("fsdp"),
            P("fsdp", None),
            P("fsdp", None),
            P(None, "fsdp"),
        ),
        check_vma=False,
    )
```
